512 devices in a mesh: pts: 128 (over y, z, core), grp: 4 (over x).
Axes of the slice: x: 4, y: 8, z: 8, core: 2. Of those that a mesh axis runs over, the one named last changes fastest.
Arguments:
- jacobian: bfloat16 [512, 6, 128, 3, 256], P(('pts', 'grp')), may hold values from -0.21875 to 0.21875
- point_blocks: float32 [512, 6, 256], P(('pts', 'grp')), may hold values from -0.5 to 4, as said below
- point_grad: bfloat16 [512, 3, 256], P(('pts', 'grp')), may hold values from -6 to 6
- camera_grad: float32 [512, 128], P(('pts', 'grp')), may hold values from -6 to 6
- damping: float32 [512, 128], replicated, may hold values from 1 to 8
- incidence: int32 [512, 6], P(('pts', 'grp')), may hold values from 0 to 511, as said below
- tile_owner: int32 [128], replicated, may hold values from 0 to 127, each once
- front_first: int32 [1], replicated, may hold values from 0 to 511
Outputs:
- tiles_out: float32 [4096, 128, 128], P(('pts', 'grp'))
- rhs_out: float32 [512, 128], P(('pts', 'grp'))
- front_panel: float32 [2304, 512], P(None, 'grp')
The draws below stay inside these ranges and needn't reach their ends.
Inputs may be any that keep to these rules, and one draw needn't show every extreme that they name: `incidence`: point cluster p names 6 different camera clusters, all among (p + t) mod 512 for t from 0 to 7. `point_blocks`: each point's diagonal entries exceed the sum of the magnitudes of the two off-diagonal entries of their row by 0.1 or more. `tile_owner`: A permutation of the pts indices.
All inputs are finite; a program needn't handle non-finite values.
Results may differ from the reference program's by a relative error of at most 0.0022.
Values sent between devices are 32-bit elements; how exact they have to be, the bound alone decides.
A program may use at most 128 MiB of HBM per device.

```python
import math
import jax
import jax.numpy as jnp
import numpy as np
from jax import lax

CR = 128
PTS = 256
TOUCH = 6
BAND = 8
FRONT = 4
PC_DEV = 1
NC = 512
NPC = 512
WIN = 18
N_PTS = 128
N_GRP = 4


def draw_incidence(key, part):
    scores = jax.random.randint(key, (NPC, BAND), 0, 1 << 20) * BAND + jnp.arange(BAND)[None, :]
    ordering = jnp.argsort(scores, axis=1)
    chosen = ordering[:, :TOUCH].astype(jnp.int32)
    owners = (jnp.arange(NPC) // PC_DEV).astype(jnp.int32)
    return jnp.mod(owners[:, None] + chosen, NC).astype(jnp.int32)


def draw_point_blocks(key, part):
    key_diag, key_cross = jax.random.split(jax.random.fold_in(key, 7))
    diagonal = jax.random.uniform(key_diag, (NPC, 3, PTS), jnp.float32, 1.5, 3.0)
    crossed = jax.random.uniform(key_cross, (NPC, 3, PTS), jnp.float32, -0.5, 0.5)
    return jnp.concatenate([diagonal, crossed], axis=1).astype(jnp.float32)


def shard_levels(key, extent, shards, least, largest):
    def one(dim, blocks):
        heights = jax.random.uniform(jax.random.fold_in(jax.random.fold_in(key, 6), dim), (blocks,), jnp.float32, least / len(shards), largest / len(shards))
        return jnp.repeat(jnp.exp(heights), extent[dim] // blocks).reshape((-1,) + (1,) * (len(extent) - dim - 1))

    level = one(*shards[0])
    for cut in shards[1:]:
        level = level * one(*cut)
    return level


def normal_values(rng, shape, scale, most, cuts=(), kind=jnp.bfloat16):
    values = scale * jax.random.normal(rng, shape, jnp.float32)
    if cuts:
        values = values * shard_levels(rng, shape, cuts, -0.22, 0.18)
    return jnp.clip(values, -most, most).astype(kind)


def setup_inputs(seed: int = 0) -> dict:
    splits = jax.random.split(jax.random.key(seed), 9)
    return {
        "jacobian": normal_values(splits[0], (NPC, TOUCH, CR, 3, PTS), (3 * PTS) ** -0.5, 0.21875, ((0, 512),)),
        "point_blocks": draw_point_blocks(jax.random.fold_in(splits[8], 71), 0),
        "point_grad": normal_values(splits[2], (NPC, 3, PTS), 1.0, 6.0, ((0, 512),)),
        "camera_grad": normal_values(splits[3], (NC, CR), 1.0, 6.0, ((0, 512),), jnp.float32),
        "damping": jnp.clip(jnp.exp(jax.random.uniform(splits[4], (NC, CR), jnp.float32, math.log(1.0), math.log(8.0))), 1.0, 8.0),
        "incidence": draw_incidence(jax.random.fold_in(splits[8], 71), 0),
        "tile_owner": jax.random.permutation(splits[6], N_PTS).astype(jnp.int32),
        "front_first": jax.random.randint(splits[7], (1,), 0, NC).astype(jnp.int32),
    }


PRECISE = lax.Precision.HIGHEST

def invert_blocks(blocks):
    diag_x = blocks[:, 0]
    diag_y = blocks[:, 1]
    diag_z = blocks[:, 2]
    cross_xy = blocks[:, 3]
    cross_xz = blocks[:, 4]
    cross_yz = blocks[:, 5]
    adj_xx = diag_y * diag_z - cross_yz * cross_yz
    adj_yy = diag_x * diag_z - cross_xz * cross_xz
    adj_zz = diag_x * diag_y - cross_xy * cross_xy
    adj_xy = cross_xz * cross_yz - cross_xy * diag_z
    adj_xz = cross_xy * cross_yz - diag_y * cross_xz
    adj_yz = cross_xy * cross_xz - diag_x * cross_yz
    determinant = diag_x * adj_xx + cross_xy * adj_xy + cross_xz * adj_xz
    inverse_det = 1.0 / determinant
    return [[adj_xx * inverse_det, adj_xy * inverse_det, adj_xz * inverse_det], [adj_xy * inverse_det, adj_yy * inverse_det, adj_yz * inverse_det], [adj_xz * inverse_det, adj_yz * inverse_det, adj_zz * inverse_det]]

def scale_jacobian(jacobian, blocks):
    inverse = invert_blocks(blocks)
    widened = jacobian.astype(jnp.float32)
    columns = []
    for target in range(3):
        summed = widened[:, :, :, 0, :] * inverse[0][target][:, None, None, :]
        summed = summed + widened[:, :, :, 1, :] * inverse[1][target][:, None, None, :]
        summed = summed + widened[:, :, :, 2, :] * inverse[2][target][:, None, None, :]
        columns.append(summed)
    return jnp.stack(columns, axis=3).astype(jnp.bfloat16)

def reference(jacobian, point_blocks, point_grad, camera_grad, damping, incidence, tile_owner, front_first):
    clusters = N_PTS * N_GRP
    point_cols = 3 * PTS
    grouped_jac = jacobian.reshape(clusters, PC_DEV, TOUCH, CR, 3, PTS)
    grouped_blocks = point_blocks.reshape(clusters, PC_DEV, 6, PTS)
    grouped_grad = point_grad.reshape(clusters, PC_DEV, 3, PTS)
    grouped_inc = incidence.reshape(clusters, PC_DEV, TOUCH)
    row_axis = np.arange(BAND)[:, None]
    take_cols = np.minimum(row_axis + np.arange(BAND)[None, :], BAND - 1)
    keep_band = jnp.asarray(row_axis + np.arange(BAND)[None, :] <= BAND - 1, jnp.float32)

    def advance(carry, inputs):
        tiles_window, rhs_window = carry
        device, jac_blk, blocks_blk, grad_blk, inc_blk = inputs
        scaled = scale_jacobian(jac_blk, blocks_blk)
        scaled_flat = scaled.reshape(PC_DEV, TOUCH, CR, point_cols).astype(jnp.float32)
        jac_flat = jac_blk.reshape(PC_DEV, TOUCH, CR, point_cols).astype(jnp.float32)
        pair_blocks = jnp.einsum('pkrx,plcx->pkrlc', scaled_flat, jac_flat, precision=PRECISE)
        pulled = jnp.einsum('pkrx,px->pkr', scaled_flat, grad_blk.reshape(PC_DEV, point_cols).astype(jnp.float32), precision=PRECISE)
        local_slot = jnp.mod(inc_blk - device, clusters)
        placing = (local_slot[:, None, :] == jnp.arange(BAND)[None, :, None]).astype(jnp.float32)
        spread = jnp.einsum('ptk,pkrlc->ptrlc', placing, pair_blocks, precision=PRECISE)
        band_grid = jnp.einsum('pql,ptrlc->tqrc', placing, spread, precision=PRECISE)
        tiles_window = tiles_window + band_grid[row_axis, take_cols] * keep_band[:, :, None, None]
        rhs_window = rhs_window + jnp.einsum('ptk,pkr->tr', placing, pulled, precision=PRECISE)
        emitted = (tiles_window[0], rhs_window[0])
        tiles_window = jnp.concatenate([tiles_window[1:], jnp.zeros((1, BAND, CR, CR), jnp.float32)], axis=0)
        rhs_window = jnp.concatenate([rhs_window[1:], jnp.zeros((1, CR), jnp.float32)], axis=0)
        return ((tiles_window, rhs_window), emitted)
    start_carry = (jnp.zeros((BAND, BAND, CR, CR), jnp.float32), jnp.zeros((BAND, CR), jnp.float32))
    devices = jnp.arange(clusters, dtype=jnp.int32)
    final_carry, emitted = lax.scan(advance, start_carry, (devices, grouped_jac, grouped_blocks, grouped_grad, grouped_inc))
    tile_rows, rhs_rows = emitted
    tile_rows = tile_rows.at[:BAND - 1].add(final_carry[0][:BAND - 1])
    rhs_rows = rhs_rows.at[:BAND - 1].add(final_carry[1][:BAND - 1])
    identity = jnp.eye(CR, dtype=jnp.float32)
    tile_rows = tile_rows.at[:, 0].add(damping[:, :, None] * identity[None, :, :])
    schur = tile_rows.reshape(BAND * clusters, CR, CR)
    reduced = camera_grad - rhs_rows
    front_start = front_first[0]
    window_base = front_start - (BAND - 1)
    row_blocks = []
    for position in range(WIN):
        member = jnp.mod(window_base + position, clusters)
        entries = []
        for front_pos in range(FRONT):
            front_id = jnp.mod(front_start + front_pos, clusters)
            ahead = jnp.mod(front_id - member, clusters)
            behind = jnp.mod(member - front_id, clusters)
            tile_fwd = schur[BAND * member + jnp.minimum(ahead, BAND - 1)]
            tile_back = schur[BAND * front_id + jnp.minimum(behind, BAND - 1)].T
            entries.append(jnp.where(ahead < BAND, tile_fwd, jnp.where(behind < BAND, tile_back, 0.0)))
        row_blocks.append(jnp.concatenate(entries, axis=1))
    window_columns = jnp.concatenate(row_blocks, axis=0)
    square = window_columns[(BAND - 1) * CR:(BAND - 1 + FRONT) * CR]
    factor = jnp.linalg.cholesky(square)
    front_panel = jax.scipy.linalg.solve_triangular(factor, window_columns.T, lower=True).T
    panel_blocks = front_panel.reshape(WIN, CR, FRONT * CR)

    def outside_front(position):
        return position < BAND - 1 or position >= BAND - 1 + FRONT
    for position in range(WIN):
        for offset in range(BAND):
            partner = position + offset
            if partner < WIN and outside_front(position) and outside_front(partner):
                member = jnp.mod(window_base + position, clusters)
                change = jnp.dot(panel_blocks[position], panel_blocks[partner].T, precision=PRECISE)
                schur = schur.at[BAND * member + offset].add(-change)
    front_ids = jnp.mod(front_start + jnp.arange(FRONT), clusters)
    solved_front = jax.scipy.linalg.solve_triangular(factor, reduced[front_ids].reshape(FRONT * CR), lower=True)
    rhs_out = reduced
    for position in range(WIN):
        member = jnp.mod(window_base + position, clusters)
        if outside_front(position):
            rhs_out = rhs_out.at[member].set(reduced[member] - jnp.dot(panel_blocks[position], solved_front, precision=PRECISE))
        else:
            front_pos = position - (BAND - 1)
            rhs_out = rhs_out.at[member].set(solved_front[front_pos * CR:(front_pos + 1) * CR])
    per_owner = BAND * clusters // N_PTS
    perm_inverse = jnp.zeros((N_PTS,), jnp.int32).at[tile_owner].set(jnp.arange(N_PTS, dtype=jnp.int32))
    arranged = schur.reshape(per_owner, N_PTS, CR, CR).transpose(1, 0, 2, 3)[perm_inverse]
    tiles_out = arranged.reshape(BAND * clusters, CR, CR)
    return (tiles_out, rhs_out, front_panel)
```

```python
import jax
import jax.numpy as jnp
from jax import lax
from jax.experimental import pallas as pl
from jax.experimental.pallas import tpu as pltpu
from jax.sharding import PartitionSpec as P

TOUCH = 6
BAND = 8
FRONT = 4
CR = 128
PTS = 256
COLS = 3 * PTS
NC = 512
WIN = 18
BLOCK = 16
N_BLOCKS = 32
ROWS = 8
BAND_TILES = 36
ITEMS = 56
MESH = pl.DeviceIdType.MESH
PRECISE = lax.Precision.HIGHEST
F32 = jnp.float32
BF16 = jnp.bfloat16


def band_index(row, offset):
    return row * BAND - row * (row - 1) // 2 + offset


def front_items():
    first = BAND - 1
    last = first + FRONT
    inside = [(i, j) for i in range(first, last) for j in range(i, last)]
    before = [(i, j) for i in range(first) for j in range(first, last) if j - i < BAND]
    after = [(i, j) for i in range(first, last) for j in range(last, WIN) if j - i < BAND]
    return inside + before + after


FRONT_ITEMS = front_items()
ITEM_OF = {pair: n for n, pair in enumerate(FRONT_ITEMS)}
RHS_ITEM = len(FRONT_ITEMS)
ZERO_TILE = 184
ZERO_ROW = 23


def dot_nt(a, b, precision=None):
    return lax.dot_general(a, b, (((1,), (1,)), ((), ())), precision=precision, preferred_element_type=F32)


def dot_nn(a, b, precision=None):
    return lax.dot_general(a, b, (((1,), (0,)), ((), ())), precision=precision, preferred_element_type=F32)


def dot_tn(a, b, precision=None):
    return lax.dot_general(a, b, (((0,), (0,)), ((), ())), precision=precision, preferred_element_type=F32)


def invert_blocks(blocks):
    diag_x, diag_y, diag_z = blocks[0:1], blocks[1:2], blocks[2:3]
    cross_xy, cross_xz, cross_yz = blocks[3:4], blocks[4:5], blocks[5:6]
    adj_xx = diag_y * diag_z - cross_yz * cross_yz
    adj_yy = diag_x * diag_z - cross_xz * cross_xz
    adj_zz = diag_x * diag_y - cross_xy * cross_xy
    adj_xy = cross_xz * cross_yz - cross_xy * diag_z
    adj_xz = cross_xy * cross_yz - diag_y * cross_xz
    adj_yz = cross_xy * cross_xz - diag_x * cross_yz
    determinant = diag_x * adj_xx + cross_xy * adj_xy + cross_xz * adj_xz
    inverse_det = 1.0 / determinant
    return [
        [adj_xx * inverse_det, adj_xy * inverse_det, adj_xz * inverse_det],
        [adj_xy * inverse_det, adj_yy * inverse_det, adj_yz * inverse_det],
        [adj_xz * inverse_det, adj_yz * inverse_det, adj_zz * inverse_det],
    ]


def pair_kernel(inc, owner, first, jac, blocks, grad, cam, damp, band, table, jac_band, scl_band):
    device = lax.axis_index("pts") * 4 + lax.axis_index("grp")
    my_block = device // BLOCK

    @pl.loop(0, 128)
    def _(r):
        table[owner[r]] = r

    start = first[0] + NC - (BAND - 1)
    for n, (row, col) in enumerate(FRONT_ITEMS):
        cluster = (start + row) % NC
        spot = (cluster % BLOCK) * BAND + (col - row)
        table[128 + n] = jnp.where(cluster // BLOCK == my_block, spot, ZERO_TILE)
    for n in range(RHS_ITEM, 64):
        table[128 + n] = ZERO_TILE
    for j in range(FRONT):
        cluster = (first[0] + j) % NC
        table[192 + j] = jnp.where(cluster // BLOCK == my_block, cluster % BLOCK, ZERO_ROW)

    inverse = invert_blocks(blocks[...])
    zero = jnp.zeros((CR, COLS), BF16)
    for a in range(BAND):
        jac_band[a] = zero
        scl_band[a] = zero
    for k in range(TOUCH):
        slot = (inc[k] + NC - device) % NC
        jac_band[slot] = jac[k]
        wide = [jac[k, :, PTS * c : PTS * (c + 1)].astype(F32) for c in range(3)]
        for c in range(3):
            summed = wide[0] * inverse[0][c]
            summed = summed + wide[1] * inverse[1][c]
            summed = summed + wide[2] * inverse[2][c]
            scl_band[slot, :, PTS * c : PTS * (c + 1)] = summed.astype(BF16)

    for a in range(BAND):
        for b in range(a, BAND):
            tile = dot_nt(scl_band[a], jac_band[b])
            if a == 0 and b == 0:
                row = lax.broadcasted_iota(jnp.int32, (CR, CR), 0)
                col = lax.broadcasted_iota(jnp.int32, (CR, CR), 1)
                tile = tile + jnp.where(row == col, damp[...], 0.0)
            band[band_index(a, b - a)] = tile
    grad8 = jnp.broadcast_to(grad[...], (16, COLS))
    rows = []
    for a in range(BAND):
        pulled = dot_nt(grad8, scl_band[a])[0:1]
        rows.append(cam[...] - pulled if a == 0 else -pulled)
    chunk = jnp.concatenate(rows, axis=0)
    for j in range(16):
        band[BAND_TILES, ROWS * j : ROWS * (j + 1)] = chunk


def exchange_kernel(
    table, band, owned, wide, mine, parts, tiles, carried, sums, sums_in, sorted_tiles, fronts, spread, gathered, sem, all_sem
):
    pts = lax.axis_index("pts")
    grp = lax.axis_index("grp")
    block = pts // 4
    low = pts % 4
    core = low % 2
    depth = low // 2
    me = 4 * low + grp
    my_rows = core * 8 + depth * 4 + grp
    row0 = pl.multiple_of(ROWS * my_rows, ROWS)

    @pl.loop(0, BLOCK)
    def _(step):
        peer = (me + step) % BLOCK
        p_low = peer // 4
        p_grp = peer % 4
        rows = (p_low % 2) * 8 + (p_low // 2) * 4 + p_grp
        src = band.at[:, pl.ds(pl.multiple_of(ROWS * rows, ROWS), ROWS), :]

        @pl.when(step == 0)
        def _():
            pltpu.make_async_copy(src, parts.at[7 + me], sem.at[1]).start()

        @pl.when(step > 0)
        def _():
            pltpu.make_async_remote_copy(
                src_ref=src,
                dst_ref=parts.at[7 + me],
                send_sem=sem.at[0],
                recv_sem=sem.at[1],
                device_id=(block * 4 + p_low, p_grp),
                device_id_type=MESH,
            ).start()

    blank = jnp.zeros((ROWS, CR), F32)

    @pl.loop(0, BAND_TILES + 1)
    def _(n):
        for q in range(7):
            parts[q, n] = blank
            parts[23 + q, n] = blank

    tiles[ZERO_TILE] = blank
    pltpu.make_async_copy(parts.at[pl.ds(7, BLOCK)], parts.at[pl.ds(7, BLOCK)], sem.at[1]).wait()

    def add_up(b):
        for d in range(BAND):
            total = parts[b + 7, band_index(0, d)]
            for a in range(1, BAND - d):
                total = total + parts[b - a + 7, band_index(a, d)]
            tiles[b * BAND + d] = total
        line = parts[b + 7, BAND_TILES, 0:1]
        for a in range(1, BAND):
            line = line + parts[b - a + 7, BAND_TILES, a : a + 1]
        sums[pl.ds(b, 1)] = line

    sums[pl.ds(16, 8)] = blank
    pl.loop(BLOCK, BLOCK + 7)(add_up)
    ahead = (block + 1) % N_BLOCKS
    carry = pltpu.make_async_remote_copy(
        src_ref=tiles.at[pl.ds(128, 56)],
        dst_ref=carried,
        send_sem=sem.at[2],
        recv_sem=sem.at[3],
        device_id=(ahead * 4 + low, grp),
        device_id_type=MESH,
    )
    carry.start()
    carry_sums = pltpu.make_async_remote_copy(
        src_ref=sums.at[pl.ds(16, 8)],
        dst_ref=sums_in,
        send_sem=sem.at[4],
        recv_sem=sem.at[5],
        device_id=(ahead * 4 + low, grp),
        device_id_type=MESH,
    )
    carry_sums.start()
    pl.loop(0, BLOCK)(add_up)
    carry.wait()
    carry_sums.wait()
    for b in range(7):
        for d in range(7 - b):
            tiles[b * BAND + d] = tiles[b * BAND + d] + carried[b * BAND + d]
    sums[0:8] = sums[0:8] + sums_in[...]
    mine[...] = jnp.broadcast_to(sums[pl.ds(me, 1)], (ROWS, CR))

    @pl.loop(0, 64)
    def _(n):
        fronts[n] = tiles[table[128 + n]]

    for j in range(FRONT):
        fronts[RHS_ITEM, j : j + 1] = sums[pl.ds(table[192 + j], 1)]

    @pl.loop(1, N_BLOCKS)
    def _(step):
        other = (block + step) % N_BLOCKS
        pltpu.make_async_remote_copy(
            src_ref=fronts.at[pl.ds(2 * other, 2)],
            dst_ref=spread.at[block],
            send_sem=sem.at[6],
            recv_sem=sem.at[7],
            device_id=(other * 4 + low, grp),
            device_id_type=MESH,
        ).start()

    spread[block] = fronts[pl.ds(2 * block, 2)]

    @pl.loop(0, 128)
    def _(o):
        sorted_tiles[o] = tiles[table[o]]

    to_grp = block // 8
    slot = block % 8

    @pl.loop(0, 128)
    def _(step):
        o = (pts + step) % 128
        here = jnp.logical_and(step == 0, to_grp == grp)
        dst = owned.at[slot, pl.ds(row0, ROWS), :]

        @pl.when(here)
        def _():
            pltpu.make_async_copy(sorted_tiles.at[o], dst, all_sem.at[1]).start()

        @pl.when(jnp.logical_not(here))
        def _():
            pltpu.make_async_remote_copy(
                src_ref=sorted_tiles.at[o],
                dst_ref=dst,
                send_sem=all_sem.at[0],
                recv_sem=all_sem.at[1],
                device_id=(o, to_grp),
                device_id_type=MESH,
            ).start()

    def await_bytes(ref, which):
        pltpu.make_async_copy(ref, ref, which).wait()

    await_bytes(spread.at[pl.ds(0, N_BLOCKS - 1)], sem.at[7])
    for i in range(2):
        total = spread[0, i]
        for b in range(1, N_BLOCKS):
            total = total + spread[b, i]
        gathered[2 * block + i] = total

    @pl.loop(1, N_BLOCKS)
    def _(step):
        other = (block + step) % N_BLOCKS
        pltpu.make_async_remote_copy(
            src_ref=gathered.at[pl.ds(2 * block, 2)],
            dst_ref=gathered.at[pl.ds(2 * block, 2)],
            send_sem=sem.at[8],
            recv_sem=sem.at[9],
            device_id=(other * 4 + low, grp),
            device_id_type=MESH,
        ).start()

    await_bytes(spread.at[pl.ds(0, N_BLOCKS - 1)], sem.at[9])

    rows8 = wide.at[:, pl.ds(row0, ROWS), :]
    for step in range(4):
        if step == 0:
            pltpu.make_async_copy(gathered.at[pl.ds(0, ITEMS)], rows8, sem.at[11]).start()
        else:
            pltpu.make_async_remote_copy(
                src_ref=gathered.at[pl.ds(0, ITEMS)],
                dst_ref=rows8,
                send_sem=sem.at[10],
                recv_sem=sem.at[11],
                device_id=(pts, (grp + step) % 4),
                device_id_type=MESH,
            ).start()
    row32 = pl.multiple_of(core * 64 + depth * 32, 32)
    await_bytes(wide.at[:, pl.ds(row32, 32), :], sem.at[11])
    along_z = pltpu.make_async_remote_copy(
        src_ref=wide.at[:, pl.ds(row32, 32), :],
        dst_ref=wide.at[:, pl.ds(row32, 32), :],
        send_sem=sem.at[12],
        recv_sem=sem.at[13],
        device_id=(pts + 2 - 4 * depth, grp),
        device_id_type=MESH,
    )
    along_z.start()
    along_z.wait()
    row64 = pl.multiple_of(core * 64, 64)
    to_core = pltpu.make_async_remote_copy(
        src_ref=wide.at[:, pl.ds(row64, 64), :],
        dst_ref=wide.at[:, pl.ds(row64, 64), :],
        send_sem=sem.at[14],
        recv_sem=sem.at[15],
        device_id=(pts + 1 - 2 * core, grp),
        device_id_type=MESH,
    )
    to_core.start()
    to_core.wait()

    await_bytes(parts.at[pl.ds(0, BLOCK - 1)], sem.at[0])
    await_bytes(spread.at[pl.ds(0, N_BLOCKS - 1)], sem.at[6])
    await_bytes(spread.at[pl.ds(0, N_BLOCKS - 1)], sem.at[8])
    await_bytes(wide.at[:, pl.ds(0, 24), :], sem.at[10])

    @pl.when(to_grp == grp)
    def _():
        await_bytes(sorted_tiles.at[pl.ds(0, 127)], all_sem.at[0])

    @pl.when(to_grp != grp)
    def _():
        await_bytes(sorted_tiles, all_sem.at[0])

    await_bytes(owned, all_sem.at[1])


def factor_rows(block, out_upper, out_inverse):
    count = CR // ROWS
    sub = lax.broadcasted_iota(jnp.int32, (ROWS, CR), 0)
    lane = lax.broadcasted_iota(jnp.int32, (ROWS, CR), 1)
    left = [block[ROWS * s : ROWS * (s + 1)] for s in range(count)]
    right = [jnp.where(sub + ROWS * s == lane, 1.0, 0.0).astype(F32) for s in range(count)]

    def across(value, column):
        return jnp.broadcast_to(value[:, column : column + 1], (ROWS, CR))

    def down(value, row):
        return jnp.broadcast_to(value[row : row + 1], (ROWS, CR))

    for b in range(count):
        base = ROWS * b
        cols = [across(left[b], base + k) for k in range(ROWS)]
        e = [[down(cols[j], i) if j <= i else None for j in range(ROWS)] for i in range(ROWS)]
        x = [down(left[b], i) for i in range(ROWS)]
        y = [down(right[b], i) for i in range(ROWS)]
        inv = []
        for j in range(ROWS):
            scale = lax.rsqrt(e[j][j])
            inv.append(scale)
            for i in range(j + 1, ROWS):
                e[i][j] = e[i][j] * scale
            x[j] = x[j] * scale
            y[j] = y[j] * scale
            for i in range(j + 1, ROWS):
                for k in range(j + 1, i + 1):
                    e[i][k] = e[i][k] - e[i][j] * e[k][j]
                x[i] = x[i] - e[i][j] * x[j]
                y[i] = y[i] - e[i][j] * y[j]
        for j in range(ROWS):
            out_upper[base + j : base + j + 1] = x[j][0:1]
            out_inverse[base + j : base + j + 1] = y[j][0:1]
        if b == count - 1:
            break
        xs = [None] * ROWS
        ys = [None] * ROWS
        for j in reversed(range(ROWS)):
            px, py = x[j], y[j]
            for i in range(j + 1, ROWS):
                px = px - e[i][j] * xs[i]
                py = py - e[i][j] * ys[i]
            xs[j] = px * inv[j]
            ys[j] = py * inv[j]
        for s in range(b + 1, count):
            ratios = [across(left[s], base + k) for k in range(ROWS)]
            for k in range(ROWS):
                left[s] = left[s] - ratios[k] * xs[k]
                right[s] = right[s] - ratios[k] * ys[k]


def front_kernel(
    table, first, owned_hbm, wide, mine, tiles_hbm, rhs, panel, square, upper, inverse, rows_of, owned, sem
):
    pts = lax.axis_index("pts")
    grp = lax.axis_index("grp")
    fetch = pltpu.make_async_copy(owned_hbm, owned, sem.at[0])
    fetch.start()
    nil = jnp.zeros((CR, CR), F32)
    lead = BAND - 1
    for i in range(FRONT):
        for j in range(i, FRONT):
            square[i, j] = wide[ITEM_OF[lead + i, lead + j]]
        inverse[i] = jnp.zeros((CR, FRONT * CR), F32)

    for i in range(WIN):
        for j in range(FRONT):
            f = lead + j
            if i < lead:
                piece = wide[ITEM_OF[i, f]] if (i, f) in ITEM_OF else nil
            elif i >= lead + FRONT:
                piece = wide[ITEM_OF[f, i]].T if (f, i) in ITEM_OF else nil
            else:
                continue
            rows_of[i, :, CR * j : CR * (j + 1)] = piece

    row = lax.broadcasted_iota(jnp.int32, (CR, CR), 0)
    col = lax.broadcasted_iota(jnp.int32, (CR, CR), 1)

    @pl.loop(0, FRONT)
    def _(k):
        at = pl.multiple_of(CR * k, CR)
        factor_rows(square[k, k], upper.at[k], upper.at[FRONT])
        own = upper[FRONT]
        upper[k] = jnp.where(row <= col, upper[k], 0.0)
        so_far = inverse[k]
        done = dot_nn(own, so_far, PRECISE)
        inverse[k] = done
        inverse[k, :, pl.ds(at, CR)] = own
        for j in range(1, FRONT):

            @pl.when(j > k)
            def _():
                square[k, j] = dot_nn(own, square[k, j], PRECISE)

        for i in range(1, FRONT):

            @pl.when(i > k)
            def _():
                lower = square[k, i]
                inverse[i] = inverse[i] - dot_tn(lower, inverse[k], PRECISE)
                for j in range(i, FRONT):
                    square[i, j] = square[i, j] - dot_tn(lower, square[k, j], PRECISE)

    part = inverse[grp]
    for i in range(WIN):
        if lead <= i < lead + FRONT:
            j = i - lead

            @pl.when(grp == j)
            def _():
                panel[CR * i : CR * (i + 1)] = upper[j].T

            @pl.when(grp < j)
            def _():
                panel[CR * i : CR * (i + 1)] = square[grp, j].T

            @pl.when(grp > j)
            def _():
                panel[CR * i : CR * (i + 1)] = nil
        else:
            panel[CR * i : CR * (i + 1)] = dot_nt(rows_of[i], part, PRECISE)

    base = first[0] + NC - lead
    device = pts * 4 + grp
    stacked = jnp.concatenate([wide[RHS_ITEM, j : j + 1] for j in range(FRONT)], axis=1)
    stacked = jnp.broadcast_to(stacked, (ROWS, FRONT * CR))
    solved = [dot_nt(stacked, inverse[j], PRECISE) for j in range(FRONT)]
    spot = (device + NC - base % NC) % NC
    rhs[...] = mine[0:1]
    for j in range(FRONT):

        @pl.when(spot == lead + j)
        def _():
            rhs[...] = solved[j][0:1]

    in_rest = jnp.logical_and(spot < WIN, jnp.logical_or(spot < lead, spot >= lead + FRONT))

    @pl.when(in_rest)
    def _():
        at = jnp.minimum(spot, WIN - 1)
        total = dot_nn(solved[0], inverse[0], PRECISE)
        for j in range(1, FRONT):
            total = total + dot_nn(solved[j], inverse[j], PRECISE)
        rhs[...] = mine[0:1] - dot_nt(total, rows_of[at], PRECISE)[0:1]

    fetch.wait()
    residue = table[pts]
    ahead = residue % BAND
    near = (residue // BAND + BLOCK - base % BLOCK) % BLOCK
    for extra in range(2):
        one = near + BLOCK * extra
        two = one + ahead
        cluster = (base + one) % NC
        fits = jnp.logical_and(two < WIN, cluster // 128 == grp)
        for p in (one, two):
            fits = jnp.logical_and(fits, jnp.logical_or(p < lead, p >= lead + FRONT))

        @pl.when(fits)
        def _():
            slot = (cluster // BLOCK) % 8
            a = rows_of[jnp.minimum(one, WIN - 1)]
            b = rows_of[jnp.minimum(two, WIN - 1)]
            change = nil
            for j in range(FRONT):
                change = change + dot_nt(dot_nt(a, inverse[j], PRECISE), dot_nt(b, inverse[j], PRECISE), PRECISE)
            owned[slot] = owned[slot] - change

    store = pltpu.make_async_copy(owned, tiles_hbm, sem.at[1])
    store.start()
    store.wait()


def vmem_spec():
    return pl.BlockSpec(memory_space=pltpu.VMEM)


def smem_spec():
    return pl.BlockSpec(memory_space=pltpu.SMEM)


def any_spec():
    return pl.BlockSpec(memory_space=pl.ANY)


def shape(*dims, dtype=F32):
    return jax.ShapeDtypeStruct(dims, dtype)


def per_device(jacobian, point_blocks, point_grad, camera_grad, damping, incidence, tile_owner, front_first):
    device = lax.axis_index("pts") * 4 + lax.axis_index("grp")
    jac = jacobian.reshape(TOUCH, CR, COLS)
    damp = lax.dynamic_slice_in_dim(damping, device, 1, 0)
    band, table = pl.pallas_call(
        pair_kernel,
        out_shape=(shape(BAND_TILES + 1, CR, CR), shape(256, dtype=jnp.int32)),
        in_specs=[smem_spec()] * 3 + [vmem_spec()] * 5,
        out_specs=(vmem_spec(), smem_spec()),
        scratch_shapes=[pltpu.VMEM((BAND, CR, COLS), BF16), pltpu.VMEM((BAND, CR, COLS), BF16)],
        compiler_params=pltpu.CompilerParams(vmem_limit_bytes=40 * 2**20),
        name="pairs",
    )(
        incidence.reshape(TOUCH),
        tile_owner,
        front_first,
        jac,
        point_blocks.reshape(6, PTS),
        point_grad.reshape(1, COLS),
        camera_grad,
        damp,
    )
    owned, wide, mine = pl.pallas_call(
        exchange_kernel,
        out_shape=(shape(8, CR, CR), shape(ITEMS, CR, CR), shape(ROWS, CR)),
        in_specs=[smem_spec(), any_spec()],
        out_specs=(any_spec(), any_spec(), vmem_spec()),
        scratch_shapes=[
            pltpu.VMEM((30, BAND_TILES + 1, ROWS, CR), F32),
            pltpu.VMEM((185, ROWS, CR), F32),
            pltpu.VMEM((56, ROWS, CR), F32),
            pltpu.VMEM((24, CR), F32),
            pltpu.VMEM((ROWS, CR), F32),
            pltpu.VMEM((128, ROWS, CR), F32),
            pltpu.VMEM((64, ROWS, CR), F32),
            pltpu.VMEM((N_BLOCKS, 2, ROWS, CR), F32),
            pltpu.VMEM((64, ROWS, CR), F32),
            pltpu.SemaphoreType.DMA((16,)),
            pltpu.SemaphoreType.DMA((2,)),
        ],
        compiler_params=pltpu.CompilerParams(vmem_limit_bytes=40 * 2**20, has_side_effects=True),
        name="exchange",
    )(table, band)
    return pl.pallas_call(
        front_kernel,
        out_shape=(shape(8, CR, CR), shape(1, CR), shape(WIN * CR, CR)),
        in_specs=[smem_spec(), smem_spec(), any_spec(), vmem_spec(), vmem_spec()],
        out_specs=(any_spec(), vmem_spec(), vmem_spec()),
        scratch_shapes=[
            pltpu.VMEM((FRONT, FRONT, CR, CR), F32),
            pltpu.VMEM((FRONT + 1, CR, CR), F32),
            pltpu.VMEM((FRONT, CR, FRONT * CR), F32),
            pltpu.VMEM((WIN, CR, FRONT * CR), F32),
            pltpu.VMEM((8, CR, CR), F32),
            pltpu.SemaphoreType.DMA((2,)),
        ],
        compiler_params=pltpu.CompilerParams(vmem_limit_bytes=40 * 2**20),
        name="front",
    )(table, front_first, owned, wide, mine)


def solution(mesh):
    in_specs = (
        P(("pts", "grp"), None, None, None, None),
        P(("pts", "grp"), None, None),
        P(("pts", "grp"), None, None),
        P(("pts", "grp"), None),
        P(),
        P(("pts", "grp"), None),
        P(),
        P(),
    )
    out_specs = (P(("pts", "grp"), None, None), P(("pts", "grp"), None), P(None, "grp"))
    return jax.shard_map(per_device, mesh=mesh, in_specs=in_specs, out_specs=out_specs, check_vma=False)
```

```python
import jax
import jax.numpy as jnp
from jax import lax
from jax.experimental import pallas as pl
from jax.experimental.pallas import tpu as pltpu
from jax.sharding import PartitionSpec as P

TOUCH = 6
BAND = 8
FRONT = 4
CR = 128
PTS = 256
COLS = 3 * PTS
NC = 512
WIN = 18
BLOCK = 16
N_BLOCKS = 32
ROWS = 8
TILES = 21
NONE = 64
INNER = 11
OUTER = 44
MESH = pl.DeviceIdType.MESH
PRECISE = lax.Precision.HIGHEST
F32 = jnp.float32
BF16 = jnp.bfloat16


def tile_index(i, j):
    return (TOUCH - 1) * i - i * (i - 1) // 2 + j


def front_items():
    first = BAND - 1
    last = first + FRONT
    inside = [(i, j) for i in range(first, last) for j in range(i, last)]
    before = [(i, j) for i in range(first) for j in range(first, last) if j - i < BAND]
    after = [(i, j) for i in range(first, last) for j in range(last, WIN) if j - i < BAND]
    return inside + before + after


FRONT_ITEMS = front_items()
RHS_ITEM = 10
OUTER_OF = {pair: n - 10 for n, pair in enumerate(FRONT_ITEMS) if n >= 10}
INNER_OF = {pair: n for n, pair in enumerate(FRONT_ITEMS) if n < 10}
ZERO_TILE = 184
ZERO_ROW = 23


def dot_nt(a, b, precision=None):
    return lax.dot_general(a, b, (((1,), (1,)), ((), ())), precision=precision, preferred_element_type=F32)


def dot_nn(a, b, precision=None):
    return lax.dot_general(a, b, (((1,), (0,)), ((), ())), precision=precision, preferred_element_type=F32)


def dot_tn(a, b, precision=None):
    return lax.dot_general(a, b, (((0,), (0,)), ((), ())), precision=precision, preferred_element_type=F32)


def invert_blocks(blocks):
    diag_x, diag_y, diag_z = blocks[0:1], blocks[1:2], blocks[2:3]
    cross_xy, cross_xz, cross_yz = blocks[3:4], blocks[4:5], blocks[5:6]
    adj_xx = diag_y * diag_z - cross_yz * cross_yz
    adj_yy = diag_x * diag_z - cross_xz * cross_xz
    adj_zz = diag_x * diag_y - cross_xy * cross_xy
    adj_xy = cross_xz * cross_yz - cross_xy * diag_z
    adj_xz = cross_xy * cross_yz - diag_y * cross_xz
    adj_yz = cross_xy * cross_xz - diag_x * cross_yz
    determinant = diag_x * adj_xx + cross_xy * adj_xy + cross_xz * adj_xz
    inverse_det = 1.0 / determinant
    return [
        [adj_xx * inverse_det, adj_xy * inverse_det, adj_xz * inverse_det],
        [adj_xy * inverse_det, adj_yy * inverse_det, adj_yz * inverse_det],
        [adj_xz * inverse_det, adj_yz * inverse_det, adj_zz * inverse_det],
    ]


def pair_kernel(inc, owner, first, jac, blocks, grad, cam, band, places, table, jac_sorted, scl_sorted):
    device = lax.axis_index("pts") * 4 + lax.axis_index("grp")
    my_block = device // BLOCK

    @pl.loop(0, 128)
    def _(r):
        table[owner[r]] = r

    start = first[0] + NC - (BAND - 1)
    for n, (row, col) in enumerate(FRONT_ITEMS):
        cluster = (start + row) % NC
        spot = (cluster % BLOCK) * BAND + (col - row)
        table[128 + n + (n >= RHS_ITEM)] = jnp.where(cluster // BLOCK == my_block, spot, ZERO_TILE)
    for n in (RHS_ITEM, *range(len(FRONT_ITEMS) + 1, 64)):
        table[128 + n] = ZERO_TILE
    for j in range(FRONT):
        cluster = (first[0] + j) % NC
        table[192 + j] = jnp.where(cluster // BLOCK == my_block, cluster % BLOCK, ZERO_ROW)

    inverse = invert_blocks(blocks[...])
    slots = [(inc[k] + NC - device) % NC for k in range(TOUCH)]
    lane = lax.broadcasted_iota(jnp.int32, (ROWS, CR), 1)
    place = jnp.full((ROWS, CR), NONE, jnp.int32)
    for k in range(TOUCH):
        rank = jnp.int32(0)
        for other in range(TOUCH):
            if other != k:
                rank = rank + (slots[other] < slots[k]).astype(jnp.int32)
        place = jnp.where(lane == slots[k], tile_index(rank, 0), place)
        place = jnp.where(lane == slots[k] + BAND, rank, place)
        jac_sorted[rank] = jac[k]
        wide = [jac[k, :, PTS * c : PTS * (c + 1)].astype(F32) for c in range(3)]
        for c in range(3):
            summed = wide[0] * inverse[0][c]
            summed = summed + wide[1] * inverse[1][c]
            summed = summed + wide[2] * inverse[2][c]
            scl_sorted[rank, :, PTS * c : PTS * (c + 1)] = summed.astype(BF16)
    places[...] = place

    for i in range(TOUCH):
        for j in range(i, TOUCH):
            band[tile_index(i, j)] = dot_nt(scl_sorted[i], jac_sorted[j])
    grad16 = jnp.broadcast_to(grad[...], (16, COLS))
    rows = [-dot_nt(grad16, scl_sorted[i])[0:1] for i in range(TOUCH)]
    chunk = jnp.concatenate([*rows, cam[...], jnp.zeros((1, CR), F32)], axis=0)
    for j in range(16):
        band[TILES, ROWS * j : ROWS * (j + 1)] = chunk


def exchange_kernel(
    table,
    band,
    places,
    damp,
    owned,
    outer,
    mine,
    stacked,
    inverse,
    across_me,
    parts,
    places_in,
    tiles,
    carried,
    sums,
    sums_in,
    sorted_tiles,
    fronts,
    spread,
    gathered,
    inner,
    square,
    upper,
    spots,
    sem,
    all_sem,
):
    pts = lax.axis_index("pts")
    grp = lax.axis_index("grp")
    block = pts // 4
    low = pts % 4
    core = low % 2
    depth = low // 2
    me = 4 * low + grp
    my_rows = core * 8 + depth * 4 + grp
    row0 = pl.multiple_of(ROWS * my_rows, ROWS)
    row32 = pl.multiple_of(core * 64 + depth * 32, 32)
    row64 = pl.multiple_of(core * 64, 64)
    z = (pts // 2) % 8
    above = pts - 2 * z + 2 * ((z + 1) % 8)
    below = pts - 2 * z + 2 * ((z + 7) % 8)
    other_core = pts + 1 - 2 * core

    def send(src, dst, out, arrive, to_pts, to_grp):
        copy = pltpu.make_async_remote_copy(
            src_ref=src, dst_ref=dst, send_sem=out, recv_sem=arrive, device_id=(to_pts, to_grp), device_id_type=MESH
        )
        copy.start()
        return copy

    def await_bytes(ref, which):
        pltpu.make_async_copy(ref, ref, which).wait()

    barrier = pltpu.get_barrier_semaphore()

    @pl.loop(1, BLOCK)
    def _(step):
        peer = (me + step) % BLOCK
        pl.semaphore_signal(barrier, inc=1, device_id=(block * 4 + peer // 4, peer % 4), device_id_type=MESH)

    @pl.loop(1, N_BLOCKS)
    def _(step):
        other = (block + step) % N_BLOCKS
        pl.semaphore_signal(barrier, inc=1, device_id=(other * 4 + low, grp), device_id_type=MESH)

    blank = jnp.zeros((ROWS, CR), F32)

    @pl.loop(0, 30)
    def _(q):
        parts[q, TILES + 1] = blank

    for q in (*range(7), *range(23, 30)):
        parts[q, TILES] = blank

        @pl.loop(0, 2 * BAND)
        def _(n):
            spots[q, n] = NONE

    tiles[ZERO_TILE] = blank
    pl.semaphore_wait(barrier, BLOCK - 1 + N_BLOCKS - 1)

    pltpu.make_async_copy(places, places_in.at[me], sem.at[23]).start()
    pltpu.make_async_copy(band.at[:, pl.ds(row0, ROWS), :], parts.at[7 + me, pl.ds(0, TILES + 1)], sem.at[1]).start()

    @pl.loop(1, BLOCK)
    def _(step):
        peer = (me + step) % BLOCK
        p_low = peer // 4
        p_grp = peer % 4
        rows = (p_low % 2) * 8 + (p_low // 2) * 4 + p_grp
        send(places, places_in.at[me], sem.at[22], sem.at[23], block * 4 + p_low, p_grp)
        src = band.at[:, pl.ds(pl.multiple_of(ROWS * rows, ROWS), ROWS), :]
        send(src, parts.at[7 + me, pl.ds(0, TILES + 1)], sem.at[0], sem.at[1], block * 4 + p_low, p_grp)

    await_bytes(places_in, sem.at[23])
    to_scalars = pltpu.make_async_copy(places_in.at[:, 0, :], spots.at[pl.ds(7, BLOCK)], sem.at[24])
    to_scalars.start()
    to_scalars.wait()
    await_bytes(parts.at[pl.ds(7, BLOCK), pl.ds(0, TILES + 1)], sem.at[1])

    sub = lax.broadcasted_iota(jnp.int32, (ROWS, CR), 0)
    lane = lax.broadcasted_iota(jnp.int32, (ROWS, CR), 1)

    def add_up(b, own):
        totals = [None] * BAND
        line = None
        for a in range(BAND):
            q = b - a + 7
            here = spots[q, a]
            for d in range(BAND - a):
                value = parts[q, jnp.minimum(here + spots[q, BAND + a + d], TILES + 1)]
                totals[d] = value if totals[d] is None else totals[d] + value
            row = parts[q, TILES, pl.ds(jnp.minimum(spots[q, BAND + a], 7), 1)]
            line = row if line is None else line + row
        if own:
            line = line + parts[b + 7, TILES, 6:7]
            totals[0] = totals[0] + jnp.where(lane == row0 + sub, damp[pl.ds(b, 1)], 0.0)
        for d in range(BAND):
            tiles[b * BAND + d] = totals[d]
        sums[pl.ds(b, 1)] = line

    sums[pl.ds(16, 8)] = blank

    @pl.loop(BLOCK, BLOCK + 7)
    def _(b):
        add_up(b, False)

    ahead = ((block + 1) % N_BLOCKS) * 4 + low
    carry = send(tiles.at[pl.ds(128, 56)], carried, sem.at[2], sem.at[3], ahead, grp)
    carry_sums = send(sums.at[pl.ds(16, 8)], sums_in, sem.at[4], sem.at[5], ahead, grp)

    @pl.loop(0, BLOCK)
    def _(b):
        add_up(b, True)

    carry.wait()
    carry_sums.wait()
    for b in range(7):
        for d in range(7 - b):
            tiles[b * BAND + d] = tiles[b * BAND + d] + carried[b * BAND + d]
    sums[0:8] = sums[0:8] + sums_in[...]
    mine[...] = jnp.broadcast_to(sums[pl.ds(me, 1)], (ROWS, CR))

    @pl.loop(0, 64)
    def _(n):
        fronts[n] = tiles[table[128 + n]]

    for j in range(FRONT):
        fronts[RHS_ITEM, j : j + 1] = sums[pl.ds(table[192 + j], 1)]

    @pl.loop(1, N_BLOCKS)
    def _(step):
        other = (block + step) % N_BLOCKS
        send(fronts.at[pl.ds(2 * other, 2)], spread.at[block], sem.at[6], sem.at[7], other * 4 + low, grp)

    spread[block] = fronts[pl.ds(2 * block, 2)]

    @pl.loop(0, 128)
    def _(o):
        sorted_tiles[o] = tiles[table[o]]

    await_bytes(spread.at[pl.ds(0, N_BLOCKS - 1)], sem.at[7])
    for i in range(2):
        total = spread[0, i]
        for b in range(1, N_BLOCKS):
            total = total + spread[b, i]
        gathered[2 * block + i] = total

    @pl.loop(1, N_BLOCKS)
    def _(step):
        other = (block + step) % N_BLOCKS
        own = gathered.at[pl.ds(2 * block, 2)]
        send(own, own, sem.at[8], sem.at[9], other * 4 + low, grp)

    await_bytes(spread.at[pl.ds(0, N_BLOCKS - 1)], sem.at[9])

    def along_x(begin, count, dst, out, arrive):
        src = gathered.at[pl.ds(begin, count)]
        rows = dst.at[:, pl.ds(row0, ROWS), :]
        pltpu.make_async_copy(src, rows, arrive).start()
        for step in range(1, 4):
            send(src, rows, out, arrive, pts, (grp + step) % 4)

    def along_z(count, dst, out, arrive):
        half = count // 2
        one = dst.at[pl.ds(0, half), pl.ds(row32, 32), :]
        two = dst.at[pl.ds(half, count - half), pl.ds(row32, 32), :]
        return send(one, one, out.at[0], arrive.at[0], above, grp), send(two, two, out.at[1], arrive.at[1], below, grp)

    def to_core(dst, out, arrive):
        half = dst.at[:, pl.ds(row64, 64), :]
        return send(half, half, out, arrive, other_core, grp)

    along_x(0, INNER, inner, sem.at[10], sem.at[11])
    along_x(INNER, OUTER, outer, sem.at[12], sem.at[13])
    await_bytes(inner.at[:, pl.ds(0, 32), :], sem.at[11])
    for copy in along_z(INNER, inner, sem.at[pl.ds(14, 2)], sem.at[pl.ds(16, 2)]):
        copy.wait()
    inner_core = to_core(inner, sem.at[18], sem.at[19])

    to_grp = block // 8
    slot = block % 8

    @pl.loop(0, 128)
    def _(step):
        o = (pts + step) % 128
        here = jnp.logical_and(step == 0, to_grp == grp)
        dst = owned.at[slot, pl.ds(row0, ROWS), :]

        @pl.when(here)
        def _():
            pltpu.make_async_copy(sorted_tiles.at[o], dst, all_sem.at[1]).start()

        @pl.when(jnp.logical_not(here))
        def _():
            send(sorted_tiles.at[o], dst, all_sem.at[0], all_sem.at[1], o, to_grp)

    inner_core.wait()
    for i in range(FRONT):
        for j in range(i, FRONT):
            square[i, j] = inner[INNER_OF[BAND - 1 + i, BAND - 1 + j]]
        inverse[i] = jnp.zeros((CR, FRONT * CR), F32)
    stacked[...] = inner[RHS_ITEM, 0:ROWS]

    row = lax.broadcasted_iota(jnp.int32, (CR, CR), 0)
    col = lax.broadcasted_iota(jnp.int32, (CR, CR), 1)

    def outer_z():
        half = OUTER // 2
        one = outer.at[pl.ds(0, half), pl.ds(row32, 32), :]
        two = outer.at[pl.ds(half, OUTER - half), pl.ds(row32, 32), :]
        pairs = ((one, 0, above), (two, 1, below))
        return [
            pltpu.make_async_remote_copy(
                src_ref=ref,
                dst_ref=ref,
                send_sem=sem.at[25 + n],
                recv_sem=sem.at[27 + n],
                device_id=(to, grp),
                device_id_type=MESH,
            )
            for ref, n, to in pairs
        ]

    def outer_core():
        half = outer.at[:, pl.ds(row64, 64), :]
        return pltpu.make_async_remote_copy(
            src_ref=half,
            dst_ref=half,
            send_sem=sem.at[20],
            recv_sem=sem.at[21],
            device_id=(other_core, grp),
            device_id_type=MESH,
        )

    @pl.loop(0, FRONT)
    def _(k):
        @pl.when(k == 1)
        def _():
            await_bytes(outer.at[:, pl.ds(0, 32), :], sem.at[13])
            for copy in outer_z():
                copy.start()

        @pl.when(k == 3)
        def _():
            for copy in outer_z():
                copy.wait()
            outer_core().start()

        at = pl.multiple_of(CR * k, CR)
        factor_rows(square[k, k], upper.at[0], upper.at[1])
        own = upper[1]
        square[k, k] = jnp.where(row <= col, upper[0], 0.0)
        done = dot_nn(own, inverse[k], PRECISE)
        inverse[k] = done
        inverse[k, :, pl.ds(at, CR)] = own
        for j in range(1, FRONT):

            @pl.when(j > k)
            def _():
                square[k, j] = dot_nn(own, square[k, j], PRECISE)

        for i in range(1, FRONT):

            @pl.when(i > k)
            def _():
                lower = square[k, i]
                inverse[i] = inverse[i] - dot_tn(lower, inverse[k], PRECISE)
                for j in range(i, FRONT):
                    square[i, j] = square[i, j] - dot_tn(lower, square[k, j], PRECISE)

    for j in range(FRONT):

        @pl.when(grp < j)
        def _():
            across_me[j] = square[grp, j].T

        @pl.when(grp == j)
        def _():
            across_me[j] = square[j, j].T

        @pl.when(grp > j)
        def _():
            across_me[j] = jnp.zeros((CR, CR), F32)

    await_bytes(places_in.at[pl.ds(0, BLOCK - 1)], sem.at[22])
    await_bytes(parts.at[pl.ds(0, BLOCK - 1), pl.ds(0, TILES + 1)], sem.at[0])
    await_bytes(spread.at[pl.ds(0, N_BLOCKS - 1)], sem.at[6])
    await_bytes(spread.at[pl.ds(0, N_BLOCKS - 1)], sem.at[8])
    await_bytes(inner.at[:, pl.ds(0, 24), :], sem.at[10])
    await_bytes(outer.at[:, pl.ds(0, 24), :], sem.at[12])

    @pl.when(to_grp == grp)
    def _():
        await_bytes(sorted_tiles.at[pl.ds(0, 127)], all_sem.at[0])

    @pl.when(to_grp != grp)
    def _():
        await_bytes(sorted_tiles, all_sem.at[0])

    await_bytes(owned, all_sem.at[1])
    outer_core().wait()


def factor_rows(block, out_upper, out_inverse):
    count = CR // ROWS
    sub = lax.broadcasted_iota(jnp.int32, (ROWS, CR), 0)
    lane = lax.broadcasted_iota(jnp.int32, (ROWS, CR), 1)
    left = [block[ROWS * s : ROWS * (s + 1)] for s in range(count)]
    right = [jnp.where(sub + ROWS * s == lane, 1.0, 0.0).astype(F32) for s in range(count)]

    def across(value, column):
        return jnp.broadcast_to(value[:, column : column + 1], (ROWS, CR))

    def down(value, row):
        return jnp.broadcast_to(value[row : row + 1], (ROWS, CR))

    for b in range(count):
        base = ROWS * b
        cols = [across(left[b], base + k) for k in range(ROWS)]
        e = [[down(cols[j], i) if j <= i else None for j in range(ROWS)] for i in range(ROWS)]
        x = [down(left[b], i) for i in range(ROWS)]
        y = [down(right[b], i) for i in range(ROWS)]
        inv = []
        for j in range(ROWS):
            scale = lax.rsqrt(e[j][j])
            inv.append(scale)
            for i in range(j + 1, ROWS):
                e[i][j] = e[i][j] * scale
            x[j] = x[j] * scale
            y[j] = y[j] * scale
            for i in range(j + 1, ROWS):
                for k in range(j + 1, i + 1):
                    e[i][k] = e[i][k] - e[i][j] * e[k][j]
                x[i] = x[i] - e[i][j] * x[j]
                y[i] = y[i] - e[i][j] * y[j]
        for j in range(ROWS):
            out_upper[base + j : base + j + 1] = x[j][0:1]
            out_inverse[base + j : base + j + 1] = y[j][0:1]
        if b == count - 1:
            break
        xs = [None] * ROWS
        ys = [None] * ROWS
        for j in reversed(range(ROWS)):
            px, py = x[j], y[j]
            for i in range(j + 1, ROWS):
                px = px - e[i][j] * xs[i]
                py = py - e[i][j] * ys[i]
            xs[j] = px * inv[j]
            ys[j] = py * inv[j]
        for s in range(b + 1, count):
            ratios = [across(left[s], base + k) for k in range(ROWS)]
            for k in range(ROWS):
                left[s] = left[s] - ratios[k] * xs[k]
                right[s] = right[s] - ratios[k] * ys[k]


def front_kernel(
    table, first, owned_hbm, outer, mine, stack, inverse, across_me, tiles_hbm, rhs, panel, rows_of, owned, sem
):
    pts = lax.axis_index("pts")
    grp = lax.axis_index("grp")
    fetch = pltpu.make_async_copy(owned_hbm, owned, sem.at[0])
    fetch.start()
    nil = jnp.zeros((CR, CR), F32)
    lead = BAND - 1

    for i in range(WIN):
        for j in range(FRONT):
            f = lead + j
            if i < lead:
                piece = outer[OUTER_OF[i, f]] if (i, f) in OUTER_OF else nil
            elif i >= lead + FRONT:
                piece = outer[OUTER_OF[f, i]].T if (f, i) in OUTER_OF else nil
            else:
                continue
            rows_of[i, :, CR * j : CR * (j + 1)] = piece

    part = inverse[grp]
    for i in range(WIN):
        if lead <= i < lead + FRONT:
            panel[CR * i : CR * (i + 1)] = across_me[i - lead]
        else:
            panel[CR * i : CR * (i + 1)] = dot_nt(rows_of[i], part, PRECISE)

    base = first[0] + NC - lead
    device = pts * 4 + grp
    stacked = jnp.concatenate([stack[j : j + 1] for j in range(FRONT)], axis=1)
    stacked = jnp.broadcast_to(stacked, (ROWS, FRONT * CR))
    solved = [dot_nt(stacked, inverse[j], PRECISE) for j in range(FRONT)]
    spot = (device + NC - base % NC) % NC
    rhs[...] = mine[0:1]
    for j in range(FRONT):

        @pl.when(spot == lead + j)
        def _():
            rhs[...] = solved[j][0:1]

    in_rest = jnp.logical_and(spot < WIN, jnp.logical_or(spot < lead, spot >= lead + FRONT))

    @pl.when(in_rest)
    def _():
        at = jnp.minimum(spot, WIN - 1)
        total = dot_nn(solved[0], inverse[0], PRECISE)
        for j in range(1, FRONT):
            total = total + dot_nn(solved[j], inverse[j], PRECISE)
        rhs[...] = mine[0:1] - dot_nt(total, rows_of[at], PRECISE)[0:1]

    fetch.wait()
    residue = table[pts]
    ahead = residue % BAND
    near = (residue // BAND + BLOCK - base % BLOCK) % BLOCK
    for extra in range(2):
        one = near + BLOCK * extra
        two = one + ahead
        cluster = (base + one) % NC
        fits = jnp.logical_and(two < WIN, cluster // 128 == grp)
        for p in (one, two):
            fits = jnp.logical_and(fits, jnp.logical_or(p < lead, p >= lead + FRONT))

        @pl.when(fits)
        def _():
            slot = (cluster // BLOCK) % 8
            a = rows_of[jnp.minimum(one, WIN - 1)]
            b = rows_of[jnp.minimum(two, WIN - 1)]
            change = nil
            for j in range(FRONT):
                change = change + dot_nt(dot_nt(a, inverse[j], PRECISE), dot_nt(b, inverse[j], PRECISE), PRECISE)
            owned[slot] = owned[slot] - change

    store = pltpu.make_async_copy(owned, tiles_hbm, sem.at[1])
    store.start()
    store.wait()


def vmem_spec():
    return pl.BlockSpec(memory_space=pltpu.VMEM)


def smem_spec():
    return pl.BlockSpec(memory_space=pltpu.SMEM)


def any_spec():
    return pl.BlockSpec(memory_space=pl.ANY)


def shape(*dims, dtype=F32):
    return jax.ShapeDtypeStruct(dims, dtype)


def per_device(jacobian, point_blocks, point_grad, camera_grad, damping, incidence, tile_owner, front_first):
    block = lax.axis_index("pts") // 4
    jac = jacobian.reshape(TOUCH, CR, COLS)
    damp = lax.dynamic_slice_in_dim(damping, block * BLOCK, BLOCK, 0)
    band, places, table = pl.pallas_call(
        pair_kernel,
        out_shape=(shape(TILES + 1, CR, CR), shape(ROWS, CR, dtype=jnp.int32), shape(256, dtype=jnp.int32)),
        in_specs=[smem_spec()] * 3 + [vmem_spec()] * 4,
        out_specs=(vmem_spec(), vmem_spec(), smem_spec()),
        scratch_shapes=[pltpu.VMEM((TOUCH, CR, COLS), BF16), pltpu.VMEM((TOUCH, CR, COLS), BF16)],
        compiler_params=pltpu.CompilerParams(vmem_limit_bytes=40 * 2**20),
        name="pairs",
    )(
        incidence.reshape(TOUCH),
        tile_owner,
        front_first,
        jac,
        point_blocks.reshape(6, PTS),
        point_grad.reshape(1, COLS),
        camera_grad,
    )
    owned, outer, mine, stack, inverse, across_me = pl.pallas_call(
        exchange_kernel,
        out_shape=(
            shape(8, CR, CR),
            shape(OUTER, CR, CR),
            shape(ROWS, CR),
            shape(ROWS, CR),
            shape(FRONT, CR, FRONT * CR),
            shape(FRONT, CR, CR),
        ),
        in_specs=[smem_spec(), any_spec(), any_spec(), vmem_spec()],
        out_specs=(any_spec(), any_spec(), vmem_spec(), vmem_spec(), vmem_spec(), vmem_spec()),
        scratch_shapes=[
            pltpu.VMEM((30, TILES + 2, ROWS, CR), F32),
            pltpu.VMEM((BLOCK, ROWS, CR), jnp.int32),
            pltpu.VMEM((185, ROWS, CR), F32),
            pltpu.VMEM((56, ROWS, CR), F32),
            pltpu.VMEM((24, CR), F32),
            pltpu.VMEM((ROWS, CR), F32),
            pltpu.VMEM((128, ROWS, CR), F32),
            pltpu.VMEM((64, ROWS, CR), F32),
            pltpu.VMEM((N_BLOCKS, 2, ROWS, CR), F32),
            pltpu.VMEM((64, ROWS, CR), F32),
            pltpu.VMEM((INNER, CR, CR), F32),
            pltpu.VMEM((FRONT, FRONT, CR, CR), F32),
            pltpu.VMEM((2, CR, CR), F32),
            pltpu.SMEM((30, CR), jnp.int32),
            pltpu.SemaphoreType.DMA((32,)),
            pltpu.SemaphoreType.DMA((2,)),
        ],
        compiler_params=pltpu.CompilerParams(
            vmem_limit_bytes=40 * 2**20, has_side_effects=True, collective_id=0
        ),
        name="exchange",
    )(table, band, places, damp)
    return pl.pallas_call(
        front_kernel,
        out_shape=(shape(8, CR, CR), shape(1, CR), shape(WIN * CR, CR)),
        in_specs=[smem_spec(), smem_spec(), any_spec()] + [vmem_spec()] * 5,
        out_specs=(any_spec(), vmem_spec(), vmem_spec()),
        scratch_shapes=[
            pltpu.VMEM((WIN, CR, FRONT * CR), F32),
            pltpu.VMEM((8, CR, CR), F32),
            pltpu.SemaphoreType.DMA((2,)),
        ],
        compiler_params=pltpu.CompilerParams(vmem_limit_bytes=40 * 2**20),
        name="front",
    )(table, front_first, owned, outer, mine, stack, inverse, across_me)


def solution(mesh):
    in_specs = (
        P(("pts", "grp"), None, None, None, None),
        P(("pts", "grp"), None, None),
        P(("pts", "grp"), None, None),
        P(("pts", "grp"), None),
        P(),
        P(("pts", "grp"), None),
        P(),
        P(),
    )
    out_specs = (P(("pts", "grp"), None, None), P(("pts", "grp"), None), P(None, "grp"))
    return jax.shard_map(per_device, mesh=mesh, in_specs=in_specs, out_specs=out_specs, check_vma=False)
```

```python
import jax
import jax.numpy as jnp
from jax import lax
from jax.experimental import pallas as pl
from jax.experimental.pallas import tpu as pltpu
from jax.sharding import PartitionSpec as P

TOUCH = 6
BAND = 8
FRONT = 4
CR = 128
PTS = 256
COLS = 3 * PTS
NC = 512
WIN = 18
BLOCK = 16
N_BLOCKS = 32
ROWS = 8
TILES = 21
NONE = 64
INNER = 11
OUTER = 44
EARLY = 28
MESH = pl.DeviceIdType.MESH
PRECISE = lax.Precision.HIGHEST
F32 = jnp.float32
BF16 = jnp.bfloat16


def tile_index(i, j):
    return (TOUCH - 1) * i - i * (i - 1) // 2 + j


def front_items():
    first = BAND - 1
    last = first + FRONT
    inside = [(i, j) for i in range(first, last) for j in range(i, last)]
    before = [(i, j) for i in range(first) for j in range(first, last) if j - i < BAND]
    after = [(i, j) for i in range(first, last) for j in range(last, WIN) if j - i < BAND]
    return inside + before + after


FRONT_ITEMS = front_items()
RHS_ITEM = 10
OUTER_OF = {pair: n - 10 for n, pair in enumerate(FRONT_ITEMS) if n >= 10}
INNER_OF = {pair: n for n, pair in enumerate(FRONT_ITEMS) if n < 10}
PLACES, PARTS, CARRY, CARRY_SUMS, SPREAD_IN, GATHER_IN, SPREAD_OUT, GATHER_OUT = range(8)
INNER_X, INNER_CORE, OUTER_X, OUTER_CORE, OWNED, SPARE, SPOTS = range(8, 15)
INNER_Z = 15
OUTER_Z = 18
FETCH = 21
OUTER_Z2 = 27
OUTER_X2 = 30
FIRST_X = 28
LINKS = 31
ZERO_TILE = 184
ZERO_ROW = 23


def dot_nt(a, b, precision=None):
    return lax.dot_general(a, b, (((1,), (1,)), ((), ())), precision=precision, preferred_element_type=F32)


def dot_three(a, b):
    a_high, b_high = a.astype(BF16), b.astype(BF16)
    a_low = (a - a_high.astype(F32)).astype(BF16)
    b_low = (b - b_high.astype(F32)).astype(BF16)
    return dot_nt(a_high, b_high) + (dot_nt(a_high, b_low) + dot_nt(a_low, b_high))


def dot_nn(a, b, precision=None):
    return lax.dot_general(a, b, (((1,), (0,)), ((), ())), precision=precision, preferred_element_type=F32)


def dot_tn(a, b, precision=None):
    return lax.dot_general(a, b, (((0,), (0,)), ((), ())), precision=precision, preferred_element_type=F32)


def invert_blocks(blocks):
    diag_x, diag_y, diag_z = blocks[0:1], blocks[1:2], blocks[2:3]
    cross_xy, cross_xz, cross_yz = blocks[3:4], blocks[4:5], blocks[5:6]
    adj_xx = diag_y * diag_z - cross_yz * cross_yz
    adj_yy = diag_x * diag_z - cross_xz * cross_xz
    adj_zz = diag_x * diag_y - cross_xy * cross_xy
    adj_xy = cross_xz * cross_yz - cross_xy * diag_z
    adj_xz = cross_xy * cross_yz - diag_y * cross_xz
    adj_yz = cross_xy * cross_xz - diag_x * cross_yz
    determinant = diag_x * adj_xx + cross_xy * adj_xy + cross_xz * adj_xz
    inverse_det = 1.0 / determinant
    return [
        [adj_xx * inverse_det, adj_xy * inverse_det, adj_xz * inverse_det],
        [adj_xy * inverse_det, adj_yy * inverse_det, adj_yz * inverse_det],
        [adj_xz * inverse_det, adj_yz * inverse_det, adj_zz * inverse_det],
    ]


def exchange_kernel(
    owners,
    first,
    inc_hbm,
    jac_hbm,
    blocks_hbm,
    grad_hbm,
    cam_hbm,
    damping,
    owned,
    outer,
    mine,
    stacked,
    inverse,
    across_me,
    jac_sorted,
    scl_sorted,
    band,
    places,
    damp,
    parts,
    places_in,
    tiles,
    carried,
    sums,
    sums_in,
    sorted_tiles,
    fronts_in,
    fronts_out,
    spread_in,
    spread_out,
    gathered_in,
    gathered_out,
    inner,
    square,
    upper,
    mine_out,
    jac,
    blocks,
    grad,
    cam,
    inc,
    spots,
    sem,
):
    pts = lax.axis_index("pts")
    grp = lax.axis_index("grp")
    device = pts * 4 + grp
    block = pts // 4
    low = pts % 4
    core = low % 2
    depth = low // 2
    me = 4 * low + grp
    my_rows = core * 8 + grp * 2 + depth
    row0 = pl.multiple_of(ROWS * my_rows, ROWS)
    row16 = pl.multiple_of(core * 64 + grp * 16, 16)
    row64 = pl.multiple_of(core * 64, 64)
    z = (pts // 2) % 8
    above = pts - 2 * z + 2 * ((z + 1) % 8)
    below = pts - 2 * z + 2 * ((z + 7) % 8)
    other_core = pts + 1 - 2 * core
    home = (11 * block) % N_BLOCKS
    home_in = home < INNER
    home_out = home < OUTER // 2

    def link(src, dst, which, to_pts, to_grp):
        return pltpu.make_async_remote_copy(
            src_ref=src,
            dst_ref=dst,
            send_sem=sem.at[2 * which],
            recv_sem=sem.at[2 * which + 1],
            device_id=(to_pts, to_grp),
            device_id_type=MESH,
        )

    def local(src, dst, which):
        return pltpu.make_async_copy(src, dst, sem.at[2 * which + 1])

    def sent(ref, which):
        pltpu.make_async_copy(ref, ref, sem.at[2 * which]).wait()

    def arrived(ref, which):
        pltpu.make_async_copy(ref, ref, sem.at[2 * which + 1]).wait()

    fetches = [
        local(inc_hbm, inc, FETCH),
        local(jac_hbm, jac, FETCH + 1),
        local(blocks_hbm, blocks, FETCH + 2),
        local(grad_hbm, grad, FETCH + 3),
        local(cam_hbm, cam, FETCH + 4),
        local(damping.at[pl.ds(pl.multiple_of(BLOCK * block, BLOCK), BLOCK)], damp, FETCH + 5),
    ]
    for fetch in fetches:
        fetch.start()

    barrier = pltpu.get_barrier_semaphore()

    @pl.loop(1, BLOCK)
    def _(step):
        peer = (me + step) % BLOCK
        pl.semaphore_signal(barrier, inc=1, device_id=(block * 4 + peer // 4, peer % 4), device_id_type=MESH)

    @pl.loop(1, N_BLOCKS)
    def _(step):
        other = (block + step) % N_BLOCKS
        pl.semaphore_signal(barrier, inc=1, device_id=(other * 4 + low, grp), device_id_type=MESH)

    for fetch in fetches:
        fetch.wait()

    sub = lax.broadcasted_iota(jnp.int32, (ROWS, CR), 0)
    lane = lax.broadcasted_iota(jnp.int32, (ROWS, CR), 1)
    slots = [(inc[0, k] + NC - device) % NC for k in range(TOUCH)]
    order = [jnp.int32(0)] * TOUCH
    place = jnp.full((ROWS, CR), NONE, jnp.int32)
    for k in range(TOUCH):
        rank = jnp.int32(0)
        for other in range(TOUCH):
            if other != k:
                rank = rank + (slots[other] < slots[k]).astype(jnp.int32)
        order = [order[r] + jnp.where(rank == r, k, 0) for r in range(TOUCH)]
        place = jnp.where(lane == slots[k], tile_index(rank, 0), place)
        place = jnp.where(lane == slots[k] + BAND, rank, place)
    places[...] = place

    factors = invert_blocks(jnp.concatenate([blocks[k] for k in range(6)], axis=0))
    for r in range(TOUCH):
        wide = []
        for c in range(3):
            piece = jac[jnp.minimum(order[r], TOUCH - 1), c]
            jac_sorted[r, :, PTS * c : PTS * (c + 1)] = piece
            wide.append(piece.astype(F32))
        for c in range(3):
            summed = wide[0] * factors[0][c]
            summed = summed + wide[1] * factors[1][c]
            summed = summed + wide[2] * factors[2][c]
            scl_sorted[r, :, PTS * c : PTS * (c + 1)] = summed.astype(BF16)

    blank = jnp.zeros((ROWS, CR), F32)

    def send_group(begin, count):
        @pl.loop(1, BLOCK)
        def _(step):
            peer = (me + step) % BLOCK
            p_low = peer // 4
            p_grp = peer % 4
            rows = pl.multiple_of(ROWS * ((p_low % 2) * 8 + p_grp * 2 + p_low // 2), ROWS)
            if begin == 0:
                link(places, places_in.at[me], PLACES, block * 4 + p_low, p_grp).start()
            src = band.at[pl.ds(begin, count), pl.ds(rows, ROWS), :]
            link(src, parts.at[7 + me, pl.ds(begin, count)], PARTS, block * 4 + p_low, p_grp).start()

        local(
            band.at[pl.ds(begin, count), pl.ds(row0, ROWS), :], parts.at[7 + me, pl.ds(begin, count)], PARTS
        ).start()

    for i in range(TOUCH):
        for j in range(i, TOUCH):
            band[tile_index(i, j)] = dot_nt(scl_sorted[i], jac_sorted[j])
        if i == 0:
            local(places, places_in.at[me], PLACES).start()
            pl.semaphore_wait(barrier, BLOCK - 1 + N_BLOCKS - 1)
            send_group(0, 6)
        if i == 1:
            send_group(6, 5)
    grad16 = [jnp.broadcast_to(grad[c : c + 1], (16, PTS)) for c in range(3)]
    grad16 = jnp.concatenate(grad16, axis=1)
    rows = [-dot_nt(grad16, scl_sorted[i])[0:1] for i in range(TOUCH)]
    chunk = jnp.concatenate([*rows, cam[...], jnp.zeros((1, CR), F32)], axis=0)
    for j in range(16):
        band[TILES, ROWS * j : ROWS * (j + 1)] = chunk
    send_group(11, TILES + 1 - 11)

    @pl.loop(0, 30)
    def _(q):
        parts[q, TILES + 1] = blank

    for q in (*range(7), *range(23, 30)):
        parts[q, TILES] = blank

        @pl.loop(0, 2 * BAND)
        def _(n):
            spots[q, n] = NONE

    tiles[ZERO_TILE] = blank
    sums[pl.ds(16, 8)] = blank
    arrived(places_in, PLACES)
    to_scalars = local(places_in.at[:, 0, :], spots.at[pl.ds(7, BLOCK)], SPOTS)
    to_scalars.start()
    to_scalars.wait()
    arrived(parts.at[pl.ds(7, BLOCK), pl.ds(0, TILES + 1)], PARTS)

    def add_up(b, own):
        totals = [None] * BAND
        line = None
        for a in range(BAND):
            q = b - a + 7
            here = spots[q, a]
            for d in range(BAND - a):
                value = parts[q, jnp.minimum(here + spots[q, BAND + a + d], TILES + 1)]
                totals[d] = value if totals[d] is None else totals[d] + value
            row = parts[q, TILES, pl.ds(jnp.minimum(spots[q, BAND + a], 7), 1)]
            line = row if line is None else line + row
        if own:
            line = line + parts[b + 7, TILES, 6:7]
            totals[0] = totals[0] + jnp.where(lane == row0 + sub, damp[pl.ds(b, 1)], 0.0)
        for d in range(BAND):
            tiles[b * BAND + d] = totals[d]
        sums[pl.ds(b, 1)] = line

    @pl.loop(BLOCK, BLOCK + 7)
    def _(b):
        add_up(b, False)

    ahead = ((block + 1) % N_BLOCKS) * 4 + low
    for b in range(7):
        src = tiles.at[pl.ds((BLOCK + b) * BAND, 7 - b)]
        link(src, carried.at[pl.ds(b * BAND, 7 - b)], CARRY, ahead, grp).start()
    carry_sums = link(sums.at[pl.ds(16, 8)], sums_in, CARRY_SUMS, ahead, grp)
    carry_sums.start()

    @pl.loop(0, BLOCK)
    def _(b):
        add_up(b, True)

    arrived(carried.at[pl.ds(0, 28)], CARRY)
    carry_sums.wait()
    for b in range(7):
        for d in range(7 - b):
            tiles[b * BAND + d] = tiles[b * BAND + d] + carried[b * BAND + d]
    sums[0:8] = sums[0:8] + sums_in[...]
    mine[...] = jnp.broadcast_to(sums[pl.ds(me, 1)], (ROWS, CR))

    window = first[0] + NC - (BAND - 1)

    def spot_of(pair):
        cluster = (window + pair[0]) % NC
        spot = (cluster % BLOCK) * BAND + (pair[1] - pair[0])
        return jnp.where(cluster // BLOCK == block, spot, ZERO_TILE)

    for n in range(RHS_ITEM):
        fronts_in[n] = tiles[spot_of(FRONT_ITEMS[n])]
    fronts_in[RHS_ITEM] = blank
    for j in range(FRONT):
        cluster = (first[0] + j) % NC
        spot = jnp.where(cluster // BLOCK == block, cluster % BLOCK, ZERO_ROW)
        fronts_in[RHS_ITEM, j : j + 1] = sums[pl.ds(spot, 1)]

    @pl.loop(1, INNER + 1)
    def _(step):
        n = (home + step) % INNER
        to = (3 * n) % N_BLOCKS

        @pl.when(to != block)
        def _():
            link(fronts_in.at[n], spread_in.at[block], SPREAD_IN, to * 4 + low, grp).start()

    for n in range(OUTER):
        fronts_out[n] = tiles[spot_of(FRONT_ITEMS[n + 10])]

    @pl.loop(1, OUTER // 2 + 1)
    def _(step):
        n = (home + step) % (OUTER // 2)
        to = (3 * n) % N_BLOCKS

        @pl.when(to != block)
        def _():
            link(fronts_out.at[pl.ds(2 * n, 2)], spread_out.at[block], SPREAD_OUT, to * 4 + low, grp).start()

    @pl.when(home_in)
    def _():
        spread_in[block] = fronts_in[home]
        arrived(spread_in.at[pl.ds(0, N_BLOCKS - 1)], SPREAD_IN)
        total = spread_in[0]
        for b in range(1, N_BLOCKS):
            total = total + spread_in[b]
        gathered_in[home] = total

        @pl.loop(1, N_BLOCKS)
        def _(step):
            other = (block + step) % N_BLOCKS
            link(gathered_in.at[home], gathered_in.at[home], GATHER_IN, other * 4 + low, grp).start()

    @pl.loop(0, 128)
    def _(o):
        sorted_tiles[o] = tiles[owners[o]]

    @pl.when(home_in)
    def _():
        arrived(gathered_in.at[pl.ds(0, INNER - 1)], GATHER_IN)

    @pl.when(jnp.logical_not(home_in))
    def _():
        arrived(gathered_in, GATHER_IN)

    def along_z(src, dst, count, which):
        half = count // 2
        one = link(src.at[pl.ds(0, half)], dst.at[pl.ds(0, half)], which, above, grp)
        two = link(src.at[pl.ds(half, count - half)], dst.at[pl.ds(half, count - half)], which + 1, below, grp)
        return one, two

    def along_x(src, dst, which):
        return [link(src, dst, which, pts, (grp + step) % 4) for step in range(1, 4)]

    def start(*copies):
        for copy in copies:
            copy.start()

    def wait(*copies):
        for copy in copies:
            copy.wait()

    def same(ref, which, to_pts):
        return link(ref, ref, which, to_pts, grp)

    inner_rows = inner.at[:, core, grp, depth]
    inner_z = (*along_z(gathered_in, inner_rows, INNER, INNER_Z), local(gathered_in, inner_rows, INNER_Z + 2))
    start(*inner_z)

    @pl.when(home_out)
    def _():
        spread_out[block] = fronts_out[pl.ds(2 * home, 2)]
        arrived(spread_out.at[pl.ds(0, N_BLOCKS - 1)], SPREAD_OUT)
        for i in range(2):
            total = spread_out[0, i]
            for b in range(1, N_BLOCKS):
                total = total + spread_out[b, i]
            mine_out[i] = total
        local(mine_out, gathered_out.at[pl.ds(2 * home, 2)], GATHER_OUT).start()

        @pl.loop(1, N_BLOCKS)
        def _(step):
            other = (block + step) % N_BLOCKS
            link(mine_out, gathered_out.at[pl.ds(2 * home, 2)], GATHER_OUT, other * 4 + low, grp).start()

    wait(*inner_z)
    inner_pair = inner.at[:, core, grp]
    start(*along_x(inner_pair, inner_pair, INNER_X))
    arrived(inner.at[:, 0, pl.ds(0, 3)], INNER_X)
    inner_core = same(inner.at[:, core], INNER_CORE, other_core)
    inner_core.start()

    first_rows = outer.at[pl.ds(0, EARLY), core, grp, depth]
    first_four = outer.at[pl.ds(0, EARLY), core, :, depth]
    other_rows = outer.at[pl.ds(EARLY, OUTER - EARLY), core, grp, depth]
    other_pair = outer.at[pl.ds(EARLY, OUTER - EARLY), core, grp]
    first_src = gathered_out.at[pl.ds(0, EARLY)]
    other_src = gathered_out.at[pl.ds(EARLY, OUTER - EARLY)]
    first_x = along_x(first_src, first_rows, OUTER_X)
    other_z = along_z(other_src, other_rows, OUTER - EARLY, OUTER_Z)
    own_rows = (local(first_src, first_rows, OUTER_X2), local(other_src, other_rows, OUTER_Z + 2))
    first_z = along_z(first_four, first_four, EARLY, OUTER_Z2)
    other_x = along_x(other_pair, other_pair, FIRST_X + 1)
    outer_core = same(outer.at[:, core], OUTER_CORE, other_core)

    def phase_one():
        arrived(gathered_out, GATHER_OUT)
        start(*first_x, *other_z, *own_rows)

    def phase_two():
        wait(*own_rows, *other_z)
        arrived(outer.at[pl.ds(0, EARLY), 0, pl.ds(0, 3), 0], OUTER_X)
        start(*first_z, *other_x)

    def phase_three():
        wait(*first_z)
        arrived(outer.at[pl.ds(EARLY, OUTER - EARLY), 0, pl.ds(0, 3)], FIRST_X + 1)
        outer_core.start()

    to_grp = block // 8
    slot = block % 8

    @pl.loop(0, 128)
    def _(step):
        o = (pts + step) % 128
        here = jnp.logical_and(step == 0, to_grp == grp)
        dst = owned.at[slot, pl.ds(row0, ROWS), :]

        @pl.when(here)
        def _():
            local(sorted_tiles.at[o], dst, OWNED).start()

        @pl.when(jnp.logical_not(here))
        def _():
            link(sorted_tiles.at[o], dst, OWNED, o, to_grp).start()

    inner_core.wait()
    for i in range(FRONT):
        for j in range(i, FRONT):
            square[i, j] = inner[INNER_OF[BAND - 1 + i, BAND - 1 + j]].reshape(CR, CR)
        for j in range(i + 1, FRONT):
            inverse[i, :, CR * j : CR * (j + 1)] = jnp.zeros((CR, CR), F32)
    stacked[...] = inner[RHS_ITEM, 0, 0, 0]

    row = lax.broadcasted_iota(jnp.int32, (CR, CR), 0)
    col = lax.broadcasted_iota(jnp.int32, (CR, CR), 1)

    def at(j):
        return slice(CR * j, CR * (j + 1))

    hooks = [{8: phase_one}, {8: phase_two}, {8: phase_three}, {}]
    for k in range(FRONT):
        factor_rows(square[k, k], upper.at[2 * k], upper.at[2 * k + 1], hooks[k])
        own = upper[2 * k + 1]
        square[k, k] = jnp.where(row <= col, upper[2 * k], 0.0)
        for j in range(k + 1, FRONT):
            square[k, j] = dot_nn(own, square[k, j], PRECISE)
        for i in range(k + 1, FRONT):
            for j in range(i, FRONT):
                square[i, j] = square[i, j] - dot_tn(square[k, i], square[k, j], PRECISE)
        for j in range(k):
            inverse[k, :, at(j)] = dot_nn(own, inverse[k, :, at(j)], PRECISE)
        inverse[k, :, at(k)] = own
        for i in range(k + 1, FRONT):
            for j in range(k + 1):
                change = dot_tn(square[k, i], inverse[k, :, at(j)], PRECISE)
                inverse[i, :, at(j)] = -change if j == k else inverse[i, :, at(j)] - change

    for j in range(FRONT):

        @pl.when(grp < j)
        def _():
            across_me[j] = square[grp, j].T

        @pl.when(grp == j)
        def _():
            across_me[j] = square[j, j].T

        @pl.when(grp > j)
        def _():
            across_me[j] = jnp.zeros((CR, CR), F32)

    sent(places_in.at[pl.ds(0, BLOCK - 1)], PLACES)
    sent(parts.at[pl.ds(0, BLOCK - 1), pl.ds(0, TILES + 1)], PARTS)
    sent(carried.at[pl.ds(0, 28)], CARRY)
    sent(inner.at[:, 0, pl.ds(0, 3)], INNER_X)
    sent(outer.at[pl.ds(0, EARLY), 0, pl.ds(0, 3), 0], OUTER_X)
    sent(outer.at[pl.ds(EARLY, OUTER - EARLY), 0, pl.ds(0, 3)], FIRST_X + 1)

    @pl.when(home_in)
    def _():
        sent(gathered_in.at[pl.ds(0, INNER - 1)], SPREAD_IN)
        sent(spread_in.at[pl.ds(0, N_BLOCKS - 1)], GATHER_IN)

    @pl.when(jnp.logical_not(home_in))
    def _():
        sent(gathered_in, SPREAD_IN)

    @pl.when(home_out)
    def _():
        sent(gathered_out.at[pl.ds(0, OUTER - 2)], SPREAD_OUT)
        sent(spread_out.at[pl.ds(0, N_BLOCKS - 1)], GATHER_OUT)

    @pl.when(jnp.logical_not(home_out))
    def _():
        sent(gathered_out, SPREAD_OUT)

    @pl.when(to_grp == grp)
    def _():
        sent(sorted_tiles.at[pl.ds(0, 127)], OWNED)

    @pl.when(to_grp != grp)
    def _():
        sent(sorted_tiles, OWNED)

    arrived(owned, OWNED)
    outer_core.wait()


def factor_rows(block, out_upper, out_inverse, hooks):
    count = CR // ROWS
    sub = lax.broadcasted_iota(jnp.int32, (ROWS, CR), 0)
    lane = lax.broadcasted_iota(jnp.int32, (ROWS, CR), 1)
    left = [block[ROWS * s : ROWS * (s + 1)] for s in range(count)]
    right = [jnp.where(sub + ROWS * s == lane, 1.0, 0.0).astype(F32) for s in range(count)]

    def across(value, column):
        return jnp.broadcast_to(value[:, column : column + 1], (ROWS, CR))

    def down(value, row):
        return jnp.broadcast_to(value[row : row + 1], (ROWS, CR))

    for b in range(count):
        if b in hooks:
            hooks[b]()
        base = ROWS * b
        cols = [across(left[b], base + k) for k in range(ROWS)]
        e = [[down(cols[j], i) if j <= i else None for j in range(ROWS)] for i in range(ROWS)]
        x = [down(left[b], i) for i in range(ROWS)]
        y = [down(right[b], i) for i in range(ROWS)]
        inv = []
        for j in range(ROWS):
            scale = lax.rsqrt(e[j][j])
            inv.append(scale)
            for i in range(j + 1, ROWS):
                e[i][j] = e[i][j] * scale
            x[j] = x[j] * scale
            y[j] = y[j] * scale
            for i in range(j + 1, ROWS):
                for k in range(j + 1, i + 1):
                    e[i][k] = e[i][k] - e[i][j] * e[k][j]
                x[i] = x[i] - e[i][j] * x[j]
                y[i] = y[i] - e[i][j] * y[j]
        for j in range(ROWS):
            out_upper[base + j : base + j + 1] = x[j][0:1]
            out_inverse[base + j : base + j + 1] = y[j][0:1]
        if b == count - 1:
            break
        xs = [None] * ROWS
        ys = [None] * ROWS
        for j in reversed(range(ROWS)):
            px, py = x[j], y[j]
            for i in range(j + 1, ROWS):
                px = px - e[i][j] * xs[i]
                py = py - e[i][j] * ys[i]
            xs[j] = px * inv[j]
            ys[j] = py * inv[j]
        for s in range(b + 1, count):
            ratios = [across(left[s], base + k) for k in range(ROWS)]
            for k in range(ROWS):
                left[s] = left[s] - ratios[k] * xs[k]
                right[s] = right[s] - ratios[k] * ys[k]


def front_kernel(
    owners,
    first,
    owned_hbm,
    outer_hbm,
    mine_hbm,
    stack_hbm,
    inverse_hbm,
    across_hbm,
    tiles_hbm,
    rhs,
    panel,
    rows_of,
    owned,
    outer,
    mine,
    stack,
    inverse,
    across_me,
    sem,
):
    pts = lax.axis_index("pts")
    grp = lax.axis_index("grp")
    fetch = pltpu.make_async_copy(owned_hbm, owned, sem.at[0])
    pairs = ((outer_hbm, outer), (inverse_hbm, inverse), (across_hbm, across_me), (mine_hbm, mine), (stack_hbm, stack))
    fetches = [pltpu.make_async_copy(src, dst, sem.at[2 + n]) for n, (src, dst) in enumerate(pairs)]
    for copy in fetches:
        copy.start()
    fetch.start()
    for copy in fetches:
        copy.wait()
    nil = jnp.zeros((CR, CR), F32)
    lead = BAND - 1

    for i in range(WIN):
        for j in range(FRONT):
            f = lead + j
            if i < lead:
                piece = outer[OUTER_OF[i, f]] if (i, f) in OUTER_OF else nil
            elif i >= lead + FRONT:
                piece = outer[OUTER_OF[f, i]].T if (f, i) in OUTER_OF else nil
            else:
                continue
            rows_of[i, :, CR * j : CR * (j + 1)] = piece

    part = inverse[grp]
    for i in range(WIN):
        if lead <= i < lead + FRONT:
            panel[CR * i : CR * (i + 1)] = across_me[i - lead]
        else:
            panel[CR * i : CR * (i + 1)] = dot_three(rows_of[i], part)

    base = first[0] + NC - lead
    device = pts * 4 + grp
    stacked = jnp.concatenate([stack[j : j + 1] for j in range(FRONT)], axis=1)
    stacked = jnp.broadcast_to(stacked, (ROWS, FRONT * CR))
    solved = [dot_nt(stacked, inverse[j], PRECISE) for j in range(FRONT)]
    spot = (device + NC - base % NC) % NC
    rhs[...] = mine[0:1]
    for j in range(FRONT):

        @pl.when(spot == lead + j)
        def _():
            rhs[...] = solved[j][0:1]

    in_rest = jnp.logical_and(spot < WIN, jnp.logical_or(spot < lead, spot >= lead + FRONT))

    @pl.when(in_rest)
    def _():
        at = jnp.minimum(spot, WIN - 1)
        total = dot_nn(solved[0], inverse[0], PRECISE)
        for j in range(1, FRONT):
            total = total + dot_nn(solved[j], inverse[j], PRECISE)
        rhs[...] = mine[0:1] - dot_nt(total, rows_of[at], PRECISE)[0:1]

    fetch.wait()
    residue = owners[pts]
    ahead = residue % BAND
    near = (residue // BAND + BLOCK - base % BLOCK) % BLOCK
    for extra in range(2):
        one = near + BLOCK * extra
        two = one + ahead
        cluster = (base + one) % NC
        fits = jnp.logical_and(two < WIN, cluster // 128 == grp)
        for p in (one, two):
            fits = jnp.logical_and(fits, jnp.logical_or(p < lead, p >= lead + FRONT))

        @pl.when(fits)
        def _():
            slot = (cluster // BLOCK) % 8
            a = rows_of[jnp.minimum(one, WIN - 1)]
            b = rows_of[jnp.minimum(two, WIN - 1)]
            change = nil
            for j in range(FRONT):
                deep = CR * (j + 1)
                row = inverse[j, :, :deep]
                change = change + dot_three(dot_three(a[:, :deep], row), dot_three(b[:, :deep], row))
            owned[slot] = owned[slot] - change

    store = pltpu.make_async_copy(owned, tiles_hbm, sem.at[1])
    store.start()
    store.wait()


def vmem_spec():
    return pl.BlockSpec(memory_space=pltpu.VMEM)


def smem_spec():
    return pl.BlockSpec(memory_space=pltpu.SMEM)


def any_spec():
    return pl.BlockSpec(memory_space=pl.ANY)


def shape(*dims, dtype=F32):
    return jax.ShapeDtypeStruct(dims, dtype)


def per_device(jacobian, point_blocks, point_grad, camera_grad, damping, incidence, tile_owner, front_first):
    index = jnp.arange(128, dtype=jnp.int32)
    owners = jnp.sum(jnp.where(tile_owner[:, None] == index[None, :], index[:, None], 0), axis=0)
    owned, outer, mine, stack, inverse, across_me = pl.pallas_call(
        exchange_kernel,
        out_shape=(
            shape(8, CR, CR),
            shape(OUTER, 2, 4, 2, ROWS, CR),
            shape(ROWS, CR),
            shape(ROWS, CR),
            shape(FRONT, CR, FRONT * CR),
            shape(FRONT, CR, CR),
        ),
        in_specs=[smem_spec()] * 2 + [pl.BlockSpec(memory_space=pltpu.HBM)] * 6,
        out_specs=(any_spec(), any_spec(), vmem_spec(), vmem_spec(), vmem_spec(), vmem_spec()),
        scratch_shapes=[
            pltpu.VMEM((TOUCH, CR, COLS), BF16),
            pltpu.VMEM((TOUCH, CR, COLS), BF16),
            pltpu.VMEM((TILES + 1, CR, CR), F32),
            pltpu.VMEM((ROWS, CR), jnp.int32),
            pltpu.VMEM((BLOCK, CR), F32),
            pltpu.VMEM((30, TILES + 2, ROWS, CR), F32),
            pltpu.VMEM((BLOCK, ROWS, CR), jnp.int32),
            pltpu.VMEM((185, ROWS, CR), F32),
            pltpu.VMEM((56, ROWS, CR), F32),
            pltpu.VMEM((24, CR), F32),
            pltpu.VMEM((ROWS, CR), F32),
            pltpu.VMEM((128, ROWS, CR), F32),
            pltpu.VMEM((INNER, ROWS, CR), F32),
            pltpu.VMEM((OUTER, ROWS, CR), F32),
            pltpu.VMEM((N_BLOCKS, ROWS, CR), F32),
            pltpu.VMEM((N_BLOCKS, 2, ROWS, CR), F32),
            pltpu.VMEM((INNER, ROWS, CR), F32),
            pltpu.VMEM((OUTER, ROWS, CR), F32),
            pltpu.VMEM((INNER, 2, 4, 2, ROWS, CR), F32),
            pltpu.VMEM((FRONT, FRONT, CR, CR), F32),
            pltpu.VMEM((2 * FRONT, CR, CR), F32),
            pltpu.VMEM((2, ROWS, CR), F32),
            pltpu.VMEM((TOUCH, 3, CR, PTS), BF16),
            pltpu.VMEM((6, 1, PTS), F32),
            pltpu.VMEM((3, PTS), BF16),
            pltpu.VMEM((1, CR), F32),
            pltpu.SMEM((1, TOUCH), jnp.int32),
            pltpu.SMEM((30, CR), jnp.int32),
            pltpu.SemaphoreType.DMA((2 * LINKS,)),
        ],
        compiler_params=pltpu.CompilerParams(
            vmem_limit_bytes=60 * 2**20, has_side_effects=True, collective_id=0
        ),
        name="exchange",
    )(
        owners,
        front_first,
        incidence,
        jacobian.reshape(TOUCH, CR, 3, PTS).transpose(0, 2, 1, 3),
        point_blocks.transpose(1, 0, 2),
        point_grad.reshape(3, PTS),
        camera_grad,
        damping,
    )
    return pl.pallas_call(
        front_kernel,
        out_shape=(shape(8, CR, CR), shape(1, CR), shape(WIN * CR, CR)),
        in_specs=[smem_spec()] * 2 + [pl.BlockSpec(memory_space=pltpu.HBM)] * 6,
        out_specs=(any_spec(), vmem_spec(), vmem_spec()),
        scratch_shapes=[
            pltpu.VMEM((WIN, CR, FRONT * CR), F32),
            pltpu.VMEM((8, CR, CR), F32),
            pltpu.VMEM((OUTER, CR, CR), F32),
            pltpu.VMEM((ROWS, CR), F32),
            pltpu.VMEM((ROWS, CR), F32),
            pltpu.VMEM((FRONT, CR, FRONT * CR), F32),
            pltpu.VMEM((FRONT, CR, CR), F32),
            pltpu.SemaphoreType.DMA((8,)),
        ],
        compiler_params=pltpu.CompilerParams(vmem_limit_bytes=60 * 2**20),
        name="front",
    )(owners, front_first, owned, outer.reshape(OUTER, CR, CR), mine, stack, inverse, across_me)


def solution(mesh):
    in_specs = (
        P(("pts", "grp"), None, None, None, None),
        P(("pts", "grp"), None, None),
        P(("pts", "grp"), None, None),
        P(("pts", "grp"), None),
        P(),
        P(("pts", "grp"), None),
        P(),
        P(),
    )
    out_specs = (P(("pts", "grp"), None, None), P(("pts", "grp"), None), P(None, "grp"))
    return jax.shard_map(per_device, mesh=mesh, in_specs=in_specs, out_specs=out_specs, check_vma=False)
```

```python
import jax
import jax.numpy as jnp
from jax import lax
from jax.experimental import pallas as pl
from jax.experimental.pallas import tpu as pltpu
from jax.sharding import PartitionSpec as P

TOUCH = 6
BAND = 8
FRONT = 4
CR = 128
PTS = 256
COLS = 3 * PTS
NC = 512
WIN = 18
BLOCK = 16
N_BLOCKS = 32
ROWS = 8
TILES = 21
NONE = 64
INNER = 11
OUTER = 44
EARLY = 28
MESH = pl.DeviceIdType.MESH
PRECISE = lax.Precision.HIGHEST
F32 = jnp.float32
BF16 = jnp.bfloat16


def tile_index(i, j):
    return (TOUCH - 1) * i - i * (i - 1) // 2 + j


def front_items():
    first = BAND - 1
    last = first + FRONT
    inside = [(i, j) for i in range(first, last) for j in range(i, last)]
    before = [(i, j) for i in range(first) for j in range(first, last) if j - i < BAND]
    after = [(i, j) for i in range(first, last) for j in range(last, WIN) if j - i < BAND]
    return inside + before + after


FRONT_ITEMS = front_items()
RHS_ITEM = 10
OUTER_OF = {pair: n - 10 for n, pair in enumerate(FRONT_ITEMS) if n >= 10}
INNER_OF = {pair: n for n, pair in enumerate(FRONT_ITEMS) if n < 10}
PLACES, PARTS, CARRY, CARRY_SUMS, SPREAD_IN, GATHER_IN, SPREAD_OUT, GATHER_OUT = range(8)
INNER_X, INNER_CORE, OUTER_X, OUTER_CORE, OWNED, SPARE, SPOTS = range(8, 15)
INNER_Z = 15
OUTER_Z = 18
FETCH = 21
OUTER_Z2 = 27
OUTER_X2 = 30
FIRST_X = 28
LINKS = 31
ZERO_TILE = 184
ZERO_ROW = 23


def dot_nt(a, b, precision=None):
    return lax.dot_general(a, b, (((1,), (1,)), ((), ())), precision=precision, preferred_element_type=F32)


def dot_three(a, b):
    a_high, b_high = a.astype(BF16), b.astype(BF16)
    a_low = (a - a_high.astype(F32)).astype(BF16)
    b_low = (b - b_high.astype(F32)).astype(BF16)
    return dot_nt(a_high, b_high) + (dot_nt(a_high, b_low) + dot_nt(a_low, b_high))


def dot_nn(a, b, precision=None):
    return lax.dot_general(a, b, (((1,), (0,)), ((), ())), precision=precision, preferred_element_type=F32)


def dot_tn(a, b, precision=None):
    return lax.dot_general(a, b, (((0,), (0,)), ((), ())), precision=precision, preferred_element_type=F32)


def invert_blocks(blocks):
    diag_x, diag_y, diag_z = blocks[0:1], blocks[1:2], blocks[2:3]
    cross_xy, cross_xz, cross_yz = blocks[3:4], blocks[4:5], blocks[5:6]
    adj_xx = diag_y * diag_z - cross_yz * cross_yz
    adj_yy = diag_x * diag_z - cross_xz * cross_xz
    adj_zz = diag_x * diag_y - cross_xy * cross_xy
    adj_xy = cross_xz * cross_yz - cross_xy * diag_z
    adj_xz = cross_xy * cross_yz - diag_y * cross_xz
    adj_yz = cross_xy * cross_xz - diag_x * cross_yz
    determinant = diag_x * adj_xx + cross_xy * adj_xy + cross_xz * adj_xz
    inverse_det = 1.0 / determinant
    return [
        [adj_xx * inverse_det, adj_xy * inverse_det, adj_xz * inverse_det],
        [adj_xy * inverse_det, adj_yy * inverse_det, adj_yz * inverse_det],
        [adj_xz * inverse_det, adj_yz * inverse_det, adj_zz * inverse_det],
    ]


def exchange_kernel(
    owners,
    first,
    inc_hbm,
    jac_hbm,
    blocks_hbm,
    grad_hbm,
    cam_hbm,
    damping,
    owned,
    outer,
    mine,
    stacked,
    inverse,
    across_me,
    jac_sorted,
    scl_sorted,
    band,
    places,
    damp,
    parts,
    places_in,
    tiles,
    carried,
    sums,
    sums_in,
    sorted_tiles,
    fronts_in,
    fronts_out,
    spread_in,
    spread_out,
    gathered_in,
    gathered_out,
    inner,
    square,
    upper,
    mine_out,
    jac,
    blocks,
    grad,
    cam,
    inc,
    spots,
    sem,
):
    pts = lax.axis_index("pts")
    grp = lax.axis_index("grp")
    device = pts * 4 + grp
    block = pts // 4
    low = pts % 4
    core = low % 2
    depth = low // 2
    me = 4 * low + grp
    my_rows = core * 8 + grp * 2 + depth
    row0 = pl.multiple_of(ROWS * my_rows, ROWS)
    row16 = pl.multiple_of(core * 64 + grp * 16, 16)
    row64 = pl.multiple_of(core * 64, 64)
    z = (pts // 2) % 8
    above = pts - 2 * z + 2 * ((z + 1) % 8)
    below = pts - 2 * z + 2 * ((z + 7) % 8)
    other_core = pts + 1 - 2 * core
    home = (11 * block) % N_BLOCKS
    home_in = home < INNER
    home_out = home < OUTER // 2

    def link(src, dst, which, to_pts, to_grp):
        return pltpu.make_async_remote_copy(
            src_ref=src,
            dst_ref=dst,
            send_sem=sem.at[2 * which],
            recv_sem=sem.at[2 * which + 1],
            device_id=(to_pts, to_grp),
            device_id_type=MESH,
        )

    def local(src, dst, which):
        return pltpu.make_async_copy(src, dst, sem.at[2 * which + 1])

    def sent(ref, which):
        pltpu.make_async_copy(ref, ref, sem.at[2 * which]).wait()

    def arrived(ref, which):
        pltpu.make_async_copy(ref, ref, sem.at[2 * which + 1]).wait()

    fetches = [
        local(inc_hbm, inc, FETCH),
        local(jac_hbm, jac, FETCH + 1),
        local(blocks_hbm, blocks, FETCH + 2),
        local(grad_hbm, grad, FETCH + 3),
        local(cam_hbm, cam, FETCH + 4),
        local(damping.at[pl.ds(pl.multiple_of(BLOCK * block, BLOCK), BLOCK)], damp, FETCH + 5),
    ]
    for fetch in fetches:
        fetch.start()

    barrier = pltpu.get_barrier_semaphore()

    @pl.loop(1, BLOCK)
    def _(step):
        peer = (me + step) % BLOCK
        pl.semaphore_signal(barrier, inc=1, device_id=(block * 4 + peer // 4, peer % 4), device_id_type=MESH)

    @pl.loop(1, N_BLOCKS)
    def _(step):
        other = (block + step) % N_BLOCKS
        pl.semaphore_signal(barrier, inc=1, device_id=(other * 4 + low, grp), device_id_type=MESH)

    for fetch in fetches:
        fetch.wait()

    sub = lax.broadcasted_iota(jnp.int32, (ROWS, CR), 0)
    lane = lax.broadcasted_iota(jnp.int32, (ROWS, CR), 1)
    slots = [(inc[0, k] + NC - device) % NC for k in range(TOUCH)]
    order = [jnp.int32(0)] * TOUCH
    place = jnp.full((ROWS, CR), NONE, jnp.int32)
    for k in range(TOUCH):
        rank = jnp.int32(0)
        for other in range(TOUCH):
            if other != k:
                rank = rank + (slots[other] < slots[k]).astype(jnp.int32)
        order = [order[r] + jnp.where(rank == r, k, 0) for r in range(TOUCH)]
        place = jnp.where(lane == slots[k], tile_index(rank, 0), place)
        place = jnp.where(lane == slots[k] + BAND, rank, place)
    places[...] = place

    factors = invert_blocks(jnp.concatenate([blocks[k] for k in range(6)], axis=0))
    for r in range(TOUCH):
        wide = []
        for c in range(3):
            piece = jac[jnp.minimum(order[r], TOUCH - 1), c]
            jac_sorted[r, :, PTS * c : PTS * (c + 1)] = piece
            wide.append(piece.astype(F32))
        for c in range(3):
            summed = wide[0] * factors[0][c]
            summed = summed + wide[1] * factors[1][c]
            summed = summed + wide[2] * factors[2][c]
            scl_sorted[r, :, PTS * c : PTS * (c + 1)] = summed.astype(BF16)

    blank = jnp.zeros((ROWS, CR), F32)

    def send_group(begin, count):
        @pl.loop(1, BLOCK)
        def _(step):
            peer = (me + step) % BLOCK
            p_low = peer // 4
            p_grp = peer % 4
            rows = pl.multiple_of(ROWS * ((p_low % 2) * 8 + p_grp * 2 + p_low // 2), ROWS)
            if begin == 0:
                link(places, places_in.at[me], PLACES, block * 4 + p_low, p_grp).start()
            src = band.at[pl.ds(begin, count), pl.ds(rows, ROWS), :]
            link(src, parts.at[7 + me, pl.ds(begin, count)], PARTS, block * 4 + p_low, p_grp).start()

        local(
            band.at[pl.ds(begin, count), pl.ds(row0, ROWS), :], parts.at[7 + me, pl.ds(begin, count)], PARTS
        ).start()

    for i in range(TOUCH):
        for j in range(i, TOUCH):
            band[tile_index(i, j)] = dot_nt(scl_sorted[i], jac_sorted[j])
        if i == 0:
            local(places, places_in.at[me], PLACES).start()
            pl.semaphore_wait(barrier, BLOCK - 1 + N_BLOCKS - 1)
            send_group(0, 6)
        if i == 1:
            send_group(6, 5)
    grad16 = [jnp.broadcast_to(grad[c : c + 1], (16, PTS)) for c in range(3)]
    grad16 = jnp.concatenate(grad16, axis=1)
    rows = [-dot_nt(grad16, scl_sorted[i])[0:1] for i in range(TOUCH)]
    chunk = jnp.concatenate([*rows, cam[...], jnp.zeros((1, CR), F32)], axis=0)
    for j in range(16):
        band[TILES, ROWS * j : ROWS * (j + 1)] = chunk
    send_group(11, TILES + 1 - 11)

    @pl.loop(0, 30)
    def _(q):
        parts[q, TILES + 1] = blank

    for q in (*range(7), *range(23, 30)):
        parts[q, TILES] = blank

        @pl.loop(0, 2 * BAND)
        def _(n):
            spots[q, n] = NONE

    tiles[ZERO_TILE] = blank
    sums[pl.ds(16, 8)] = blank
    arrived(places_in, PLACES)
    to_scalars = local(places_in.at[:, 0, :], spots.at[pl.ds(7, BLOCK)], SPOTS)
    to_scalars.start()
    to_scalars.wait()
    arrived(parts.at[pl.ds(7, BLOCK), pl.ds(0, TILES + 1)], PARTS)

    def add_up(b, own):
        totals = [None] * BAND
        line = None
        for a in range(BAND):
            q = b - a + 7
            here = spots[q, a]
            for d in range(BAND - a):
                value = parts[q, jnp.minimum(here + spots[q, BAND + a + d], TILES + 1)]
                totals[d] = value if totals[d] is None else totals[d] + value
            row = parts[q, TILES, pl.ds(jnp.minimum(spots[q, BAND + a], 7), 1)]
            line = row if line is None else line + row
        if own:
            line = line + parts[b + 7, TILES, 6:7]
            totals[0] = totals[0] + jnp.where(lane == row0 + sub, damp[pl.ds(b, 1)], 0.0)
        for d in range(BAND):
            tiles[b * BAND + d] = totals[d]
        sums[pl.ds(b, 1)] = line

    @pl.loop(BLOCK, BLOCK + 7)
    def _(b):
        add_up(b, False)

    ahead = ((block + 1) % N_BLOCKS) * 4 + low
    for b in range(7):
        src = tiles.at[pl.ds((BLOCK + b) * BAND, 7 - b)]
        link(src, carried.at[pl.ds(b * BAND, 7 - b)], CARRY, ahead, grp).start()
    carry_sums = link(sums.at[pl.ds(16, 8)], sums_in, CARRY_SUMS, ahead, grp)
    carry_sums.start()

    @pl.loop(0, BLOCK)
    def _(b):
        add_up(b, True)

    arrived(carried.at[pl.ds(0, 28)], CARRY)
    carry_sums.wait()
    for b in range(7):
        for d in range(7 - b):
            tiles[b * BAND + d] = tiles[b * BAND + d] + carried[b * BAND + d]
    sums[0:8] = sums[0:8] + sums_in[...]
    mine[...] = jnp.broadcast_to(sums[pl.ds(me, 1)], (ROWS, CR))

    window = first[0] + NC - (BAND - 1)

    def spot_of(pair):
        cluster = (window + pair[0]) % NC
        spot = (cluster % BLOCK) * BAND + (pair[1] - pair[0])
        return jnp.where(cluster // BLOCK == block, spot, ZERO_TILE)

    for n in range(RHS_ITEM):
        fronts_in[n] = tiles[spot_of(FRONT_ITEMS[n])]
    fronts_in[RHS_ITEM] = blank
    for j in range(FRONT):
        cluster = (first[0] + j) % NC
        spot = jnp.where(cluster // BLOCK == block, cluster % BLOCK, ZERO_ROW)
        fronts_in[RHS_ITEM, j : j + 1] = sums[pl.ds(spot, 1)]

    @pl.loop(1, INNER + 1)
    def _(step):
        n = (home + step) % INNER
        to = (3 * n) % N_BLOCKS

        @pl.when(to != block)
        def _():
            link(fronts_in.at[n], spread_in.at[block], SPREAD_IN, to * 4 + low, grp).start()

    for n in range(OUTER):
        fronts_out[n] = tiles[spot_of(FRONT_ITEMS[n + 10])]

    @pl.loop(1, OUTER // 2 + 1)
    def _(step):
        n = (home + step) % (OUTER // 2)
        to = (3 * n) % N_BLOCKS

        @pl.when(to != block)
        def _():
            link(fronts_out.at[pl.ds(2 * n, 2)], spread_out.at[block], SPREAD_OUT, to * 4 + low, grp).start()

    @pl.when(home_in)
    def _():
        spread_in[block] = fronts_in[home]
        arrived(spread_in.at[pl.ds(0, N_BLOCKS - 1)], SPREAD_IN)
        total = spread_in[0]
        for b in range(1, N_BLOCKS):
            total = total + spread_in[b]
        gathered_in[home] = total

        @pl.loop(1, N_BLOCKS)
        def _(step):
            other = (block + step) % N_BLOCKS
            link(gathered_in.at[home], gathered_in.at[home], GATHER_IN, other * 4 + low, grp).start()

    @pl.loop(0, 128)
    def _(o):
        sorted_tiles[o] = tiles[owners[o]]

    @pl.when(home_in)
    def _():
        arrived(gathered_in.at[pl.ds(0, INNER - 1)], GATHER_IN)

    @pl.when(jnp.logical_not(home_in))
    def _():
        arrived(gathered_in, GATHER_IN)

    def along_z(src, dst, count, which):
        half = count // 2
        one = link(src.at[pl.ds(0, half)], dst.at[pl.ds(0, half)], which, above, grp)
        two = link(src.at[pl.ds(half, count - half)], dst.at[pl.ds(half, count - half)], which + 1, below, grp)
        return one, two

    def along_x(src, dst, which):
        return [link(src, dst, which, pts, (grp + step) % 4) for step in range(1, 4)]

    def start(*copies):
        for copy in copies:
            copy.start()

    def wait(*copies):
        for copy in copies:
            copy.wait()

    def same(ref, which, to_pts):
        return link(ref, ref, which, to_pts, grp)

    inner_rows = inner.at[:, core, grp, depth]
    inner_z = (*along_z(gathered_in, inner_rows, INNER, INNER_Z), local(gathered_in, inner_rows, INNER_Z + 2))
    start(*inner_z)

    @pl.when(home_out)
    def _():
        spread_out[block] = fronts_out[pl.ds(2 * home, 2)]
        arrived(spread_out.at[pl.ds(0, N_BLOCKS - 1)], SPREAD_OUT)
        for i in range(2):
            total = spread_out[0, i]
            for b in range(1, N_BLOCKS):
                total = total + spread_out[b, i]
            mine_out[i] = total
        local(mine_out, gathered_out.at[pl.ds(2 * home, 2)], GATHER_OUT).start()

        @pl.loop(1, N_BLOCKS)
        def _(step):
            other = (block + step) % N_BLOCKS
            link(mine_out, gathered_out.at[pl.ds(2 * home, 2)], GATHER_OUT, other * 4 + low, grp).start()

    wait(*inner_z)
    inner_pair = inner.at[:, core, grp]
    start(*along_x(inner_pair, inner_pair, INNER_X))
    arrived(inner.at[:, 0, pl.ds(0, 3)], INNER_X)
    inner_core = same(inner.at[:, core], INNER_CORE, other_core)
    inner_core.start()

    first_rows = outer.at[pl.ds(0, EARLY), core, grp, depth]
    first_four = outer.at[pl.ds(0, EARLY), core, :, depth]
    other_rows = outer.at[pl.ds(EARLY, OUTER - EARLY), core, grp, depth]
    other_pair = outer.at[pl.ds(EARLY, OUTER - EARLY), core, grp]
    first_src = gathered_out.at[pl.ds(0, EARLY)]
    other_src = gathered_out.at[pl.ds(EARLY, OUTER - EARLY)]
    first_x = along_x(first_src, first_rows, OUTER_X)
    other_z = along_z(other_src, other_rows, OUTER - EARLY, OUTER_Z)
    own_rows = (local(first_src, first_rows, OUTER_X2), local(other_src, other_rows, OUTER_Z + 2))
    first_z = along_z(first_four, first_four, EARLY, OUTER_Z2)
    other_x = along_x(other_pair, other_pair, FIRST_X + 1)
    outer_core = same(outer.at[:, core], OUTER_CORE, other_core)

    def phase_one():
        arrived(gathered_out, GATHER_OUT)
        start(*first_x, *other_z, *own_rows)

    def phase_two():
        wait(*own_rows, *other_z)
        arrived(outer.at[pl.ds(0, EARLY), 0, pl.ds(0, 3), 0], OUTER_X)
        start(*first_z, *other_x)

    def phase_three():
        wait(*first_z)
        arrived(outer.at[pl.ds(EARLY, OUTER - EARLY), 0, pl.ds(0, 3)], FIRST_X + 1)
        outer_core.start()

    to_grp = block // 8
    slot = block % 8

    @pl.loop(0, 128)
    def _(step):
        o = (pts + step) % 128
        here = jnp.logical_and(step == 0, to_grp == grp)
        dst = owned.at[slot, pl.ds(row0, ROWS), :]

        @pl.when(here)
        def _():
            local(sorted_tiles.at[o], dst, OWNED).start()

        @pl.when(jnp.logical_not(here))
        def _():
            link(sorted_tiles.at[o], dst, OWNED, o, to_grp).start()

    inner_core.wait()
    for i in range(FRONT):
        for j in range(i, FRONT):
            square[i, j] = inner[INNER_OF[BAND - 1 + i, BAND - 1 + j]].reshape(CR, CR)
        for j in range(i + 1, FRONT):
            inverse[i, :, CR * j : CR * (j + 1)] = jnp.zeros((CR, CR), F32)
    stacked[...] = inner[RHS_ITEM, 0, 0, 0]

    row = lax.broadcasted_iota(jnp.int32, (CR, CR), 0)
    col = lax.broadcasted_iota(jnp.int32, (CR, CR), 1)

    def at(j):
        return slice(CR * j, CR * (j + 1))

    hooks = [{10: phase_one}, {12: phase_two}, {}, {4: phase_three}]
    for k in range(FRONT):
        factor_rows(square[k, k], upper.at[2 * k], upper.at[2 * k + 1], hooks[k])
        own = upper[2 * k + 1]
        square[k, k] = jnp.where(row <= col, upper[2 * k], 0.0)
        for j in range(k + 1, FRONT):
            square[k, j] = dot_nn(own, square[k, j], PRECISE)
        for i in range(k + 1, FRONT):
            for j in range(i, FRONT):
                square[i, j] = square[i, j] - dot_tn(square[k, i], square[k, j], PRECISE)
        for j in range(k):
            inverse[k, :, at(j)] = dot_nn(own, inverse[k, :, at(j)], PRECISE)
        inverse[k, :, at(k)] = own
        for i in range(k + 1, FRONT):
            for j in range(k + 1):
                change = dot_tn(square[k, i], inverse[k, :, at(j)], PRECISE)
                inverse[i, :, at(j)] = -change if j == k else inverse[i, :, at(j)] - change

    for j in range(FRONT):

        @pl.when(grp < j)
        def _():
            across_me[j] = square[grp, j].T

        @pl.when(grp == j)
        def _():
            across_me[j] = square[j, j].T

        @pl.when(grp > j)
        def _():
            across_me[j] = jnp.zeros((CR, CR), F32)

    sent(places_in.at[pl.ds(0, BLOCK - 1)], PLACES)
    sent(parts.at[pl.ds(0, BLOCK - 1), pl.ds(0, TILES + 1)], PARTS)
    sent(carried.at[pl.ds(0, 28)], CARRY)
    sent(inner.at[:, 0, pl.ds(0, 3)], INNER_X)
    sent(outer.at[pl.ds(0, EARLY), 0, pl.ds(0, 3), 0], OUTER_X)
    sent(outer.at[pl.ds(EARLY, OUTER - EARLY), 0, pl.ds(0, 3)], FIRST_X + 1)

    @pl.when(home_in)
    def _():
        sent(gathered_in.at[pl.ds(0, INNER - 1)], SPREAD_IN)
        sent(spread_in.at[pl.ds(0, N_BLOCKS - 1)], GATHER_IN)

    @pl.when(jnp.logical_not(home_in))
    def _():
        sent(gathered_in, SPREAD_IN)

    @pl.when(home_out)
    def _():
        sent(gathered_out.at[pl.ds(0, OUTER - 2)], SPREAD_OUT)
        sent(spread_out.at[pl.ds(0, N_BLOCKS - 1)], GATHER_OUT)

    @pl.when(jnp.logical_not(home_out))
    def _():
        sent(gathered_out, SPREAD_OUT)

    @pl.when(to_grp == grp)
    def _():
        sent(sorted_tiles.at[pl.ds(0, 127)], OWNED)

    @pl.when(to_grp != grp)
    def _():
        sent(sorted_tiles, OWNED)

    arrived(owned, OWNED)
    outer_core.wait()


def factor_rows(block, out_upper, out_inverse, hooks):
    count = CR // ROWS
    sub = lax.broadcasted_iota(jnp.int32, (ROWS, CR), 0)
    lane = lax.broadcasted_iota(jnp.int32, (ROWS, CR), 1)
    left = [block[ROWS * s : ROWS * (s + 1)] for s in range(count)]
    right = [jnp.where(sub + ROWS * s == lane, 1.0, 0.0).astype(F32) for s in range(count)]

    def across(value, column):
        return jnp.broadcast_to(value[:, column : column + 1], (ROWS, CR))

    def down(value, row):
        return jnp.broadcast_to(value[row : row + 1], (ROWS, CR))

    cols = [across(left[0], k) for k in range(ROWS)]
    for b in range(count):
        if b in hooks:
            hooks[b]()
        base = ROWS * b
        last = b == count - 1
        e = [[down(cols[j], i) if j <= i else None for j in range(ROWS)] for i in range(ROWS)]
        x = [down(left[b], i) for i in range(ROWS)]
        y = [down(right[b], i) for i in range(ROWS)]
        if not last:
            near = [across(left[b + 1], base + k) for k in range(ROWS)]
            cols = [across(left[b + 1], base + ROWS + k) for k in range(ROWS)]
        inv = []
        for j in range(0, ROWS, 2):
            p, q, r = e[j][j], e[j + 1][j], e[j + 1][j + 1]
            one = lax.rsqrt(p)
            two = one * lax.rsqrt(p * r - q * q)
            inv += [one, p * two]
            e[j + 1][j] = q * one

            def pair(u, v):
                return u * one, (p * v - q * u) * two

            for i in range(j + 2, ROWS):
                e[i][j], e[i][j + 1] = pair(e[i][j], e[i][j + 1])
            for i in range(j + 2, ROWS):
                for k in range(j + 2, i + 1):
                    e[i][k] = e[i][k] - (e[i][j] * e[k][j] + e[i][j + 1] * e[k][j + 1])
            x[j], x[j + 1] = pair(x[j], x[j + 1])
            y[j], y[j + 1] = pair(y[j], y[j + 1])
            for i in range(j + 2, ROWS):
                x[i] = x[i] - (e[i][j] * x[j] + e[i][j + 1] * x[j + 1])
                y[i] = y[i] - (e[i][j] * y[j] + e[i][j + 1] * y[j + 1])
            if not last:
                m, n = pair(near[j], near[j + 1])
                for k in range(j + 2, ROWS):
                    near[k] = near[k] - (m * e[k][j] + n * e[k][j + 1])
                for k in range(ROWS):
                    cols[k] = cols[k] - (m * down(m, k) + n * down(n, k))
                left[b + 1] = left[b + 1] - (m * x[j] + n * x[j + 1])
                right[b + 1] = right[b + 1] - (m * y[j] + n * y[j + 1])
        for j in range(ROWS):
            out_upper[base + j : base + j + 1] = x[j][0:1]
            out_inverse[base + j : base + j + 1] = y[j][0:1]
        if b >= count - 2:
            continue
        xs = [None] * ROWS
        ys = [None] * ROWS
        for j in reversed(range(ROWS)):
            px, py = x[j], y[j]
            for i in range(j + 1, ROWS):
                px = px - e[i][j] * xs[i]
                py = py - e[i][j] * ys[i]
            xs[j] = px * inv[j]
            ys[j] = py * inv[j]
        for s in range(b + 2, count):
            ratios = [across(left[s], base + k) for k in range(ROWS)]
            for k in range(ROWS):
                left[s] = left[s] - ratios[k] * xs[k]
                right[s] = right[s] - ratios[k] * ys[k]


def front_kernel(
    owners,
    first,
    owned_hbm,
    outer_hbm,
    mine_hbm,
    stack_hbm,
    inverse_hbm,
    across_hbm,
    tiles_hbm,
    rhs,
    panel,
    rows_of,
    owned,
    outer,
    mine,
    stack,
    inverse,
    across_me,
    sem,
):
    pts = lax.axis_index("pts")
    grp = lax.axis_index("grp")
    fetch = pltpu.make_async_copy(owned_hbm, owned, sem.at[0])
    pairs = ((outer_hbm, outer), (inverse_hbm, inverse), (across_hbm, across_me), (mine_hbm, mine), (stack_hbm, stack))
    fetches = [pltpu.make_async_copy(src, dst, sem.at[2 + n]) for n, (src, dst) in enumerate(pairs)]
    for copy in fetches:
        copy.start()
    fetch.start()
    for copy in fetches:
        copy.wait()
    nil = jnp.zeros((CR, CR), F32)
    lead = BAND - 1

    for i in range(WIN):
        for j in range(FRONT):
            f = lead + j
            if i < lead:
                piece = outer[OUTER_OF[i, f]] if (i, f) in OUTER_OF else nil
            elif i >= lead + FRONT:
                piece = outer[OUTER_OF[f, i]].T if (f, i) in OUTER_OF else nil
            else:
                continue
            rows_of[i, :, CR * j : CR * (j + 1)] = piece

    part = inverse[grp]
    for i in range(WIN):
        if lead <= i < lead + FRONT:
            panel[CR * i : CR * (i + 1)] = across_me[i - lead]
        else:
            panel[CR * i : CR * (i + 1)] = dot_three(rows_of[i], part)

    base = first[0] + NC - lead
    device = pts * 4 + grp
    stacked = jnp.concatenate([stack[j : j + 1] for j in range(FRONT)], axis=1)
    stacked = jnp.broadcast_to(stacked, (ROWS, FRONT * CR))
    solved = [dot_nt(stacked, inverse[j], PRECISE) for j in range(FRONT)]
    spot = (device + NC - base % NC) % NC
    rhs[...] = mine[0:1]
    for j in range(FRONT):

        @pl.when(spot == lead + j)
        def _():
            rhs[...] = solved[j][0:1]

    in_rest = jnp.logical_and(spot < WIN, jnp.logical_or(spot < lead, spot >= lead + FRONT))

    @pl.when(in_rest)
    def _():
        at = jnp.minimum(spot, WIN - 1)
        total = dot_nn(solved[0], inverse[0], PRECISE)
        for j in range(1, FRONT):
            total = total + dot_nn(solved[j], inverse[j], PRECISE)
        rhs[...] = mine[0:1] - dot_nt(total, rows_of[at], PRECISE)[0:1]

    fetch.wait()
    residue = owners[pts]
    ahead = residue % BAND
    near = (residue // BAND + BLOCK - base % BLOCK) % BLOCK
    for extra in range(2):
        one = near + BLOCK * extra
        two = one + ahead
        cluster = (base + one) % NC
        fits = jnp.logical_and(two < WIN, cluster // 128 == grp)
        for p in (one, two):
            fits = jnp.logical_and(fits, jnp.logical_or(p < lead, p >= lead + FRONT))

        @pl.when(fits)
        def _():
            slot = (cluster // BLOCK) % 8
            a = rows_of[jnp.minimum(one, WIN - 1)]
            b = rows_of[jnp.minimum(two, WIN - 1)]
            change = nil
            for j in range(FRONT):
                deep = CR * (j + 1)
                row = inverse[j, :, :deep]
                change = change + dot_three(dot_three(a[:, :deep], row), dot_three(b[:, :deep], row))
            owned[slot] = owned[slot] - change

    store = pltpu.make_async_copy(owned, tiles_hbm, sem.at[1])
    store.start()
    store.wait()


def vmem_spec():
    return pl.BlockSpec(memory_space=pltpu.VMEM)


def smem_spec():
    return pl.BlockSpec(memory_space=pltpu.SMEM)


def any_spec():
    return pl.BlockSpec(memory_space=pl.ANY)


def shape(*dims, dtype=F32):
    return jax.ShapeDtypeStruct(dims, dtype)


def per_device(jacobian, point_blocks, point_grad, camera_grad, damping, incidence, tile_owner, front_first):
    index = jnp.arange(128, dtype=jnp.int32)
    owners = jnp.sum(jnp.where(tile_owner[:, None] == index[None, :], index[:, None], 0), axis=0)
    owned, outer, mine, stack, inverse, across_me = pl.pallas_call(
        exchange_kernel,
        out_shape=(
            shape(8, CR, CR),
            shape(OUTER, 2, 4, 2, ROWS, CR),
            shape(ROWS, CR),
            shape(ROWS, CR),
            shape(FRONT, CR, FRONT * CR),
            shape(FRONT, CR, CR),
        ),
        in_specs=[smem_spec()] * 2 + [pl.BlockSpec(memory_space=pltpu.HBM)] * 6,
        out_specs=(any_spec(), any_spec(), vmem_spec(), vmem_spec(), vmem_spec(), vmem_spec()),
        scratch_shapes=[
            pltpu.VMEM((TOUCH, CR, COLS), BF16),
            pltpu.VMEM((TOUCH, CR, COLS), BF16),
            pltpu.VMEM((TILES + 1, CR, CR), F32),
            pltpu.VMEM((ROWS, CR), jnp.int32),
            pltpu.VMEM((BLOCK, CR), F32),
            pltpu.VMEM((30, TILES + 2, ROWS, CR), F32),
            pltpu.VMEM((BLOCK, ROWS, CR), jnp.int32),
            pltpu.VMEM((185, ROWS, CR), F32),
            pltpu.VMEM((56, ROWS, CR), F32),
            pltpu.VMEM((24, CR), F32),
            pltpu.VMEM((ROWS, CR), F32),
            pltpu.VMEM((128, ROWS, CR), F32),
            pltpu.VMEM((INNER, ROWS, CR), F32),
            pltpu.VMEM((OUTER, ROWS, CR), F32),
            pltpu.VMEM((N_BLOCKS, ROWS, CR), F32),
            pltpu.VMEM((N_BLOCKS, 2, ROWS, CR), F32),
            pltpu.VMEM((INNER, ROWS, CR), F32),
            pltpu.VMEM((OUTER, ROWS, CR), F32),
            pltpu.VMEM((INNER, 2, 4, 2, ROWS, CR), F32),
            pltpu.VMEM((FRONT, FRONT, CR, CR), F32),
            pltpu.VMEM((2 * FRONT, CR, CR), F32),
            pltpu.VMEM((2, ROWS, CR), F32),
            pltpu.VMEM((TOUCH, 3, CR, PTS), BF16),
            pltpu.VMEM((6, 1, PTS), F32),
            pltpu.VMEM((3, PTS), BF16),
            pltpu.VMEM((1, CR), F32),
            pltpu.SMEM((1, TOUCH), jnp.int32),
            pltpu.SMEM((30, CR), jnp.int32),
            pltpu.SemaphoreType.DMA((2 * LINKS,)),
        ],
        compiler_params=pltpu.CompilerParams(
            vmem_limit_bytes=60 * 2**20, has_side_effects=True, collective_id=0
        ),
        name="exchange",
    )(
        owners,
        front_first,
        incidence,
        jacobian.reshape(TOUCH, CR, 3, PTS).transpose(0, 2, 1, 3),
        point_blocks.transpose(1, 0, 2),
        point_grad.reshape(3, PTS),
        camera_grad,
        damping,
    )
    return pl.pallas_call(
        front_kernel,
        out_shape=(shape(8, CR, CR), shape(1, CR), shape(WIN * CR, CR)),
        in_specs=[smem_spec()] * 2 + [pl.BlockSpec(memory_space=pltpu.HBM)] * 6,
        out_specs=(any_spec(), vmem_spec(), vmem_spec()),
        scratch_shapes=[
            pltpu.VMEM((WIN, CR, FRONT * CR), F32),
            pltpu.VMEM((8, CR, CR), F32),
            pltpu.VMEM((OUTER, CR, CR), F32),
            pltpu.VMEM((ROWS, CR), F32),
            pltpu.VMEM((ROWS, CR), F32),
            pltpu.VMEM((FRONT, CR, FRONT * CR), F32),
            pltpu.VMEM((FRONT, CR, CR), F32),
            pltpu.SemaphoreType.DMA((8,)),
        ],
        compiler_params=pltpu.CompilerParams(vmem_limit_bytes=60 * 2**20),
        name="front",
    )(owners, front_first, owned, outer.reshape(OUTER, CR, CR), mine, stack, inverse, across_me)


def solution(mesh):
    in_specs = (
        P(("pts", "grp"), None, None, None, None),
        P(("pts", "grp"), None, None),
        P(("pts", "grp"), None, None),
        P(("pts", "grp"), None),
        P(),
        P(("pts", "grp"), None),
        P(),
        P(),
    )
    out_specs = (P(("pts", "grp"), None, None), P(("pts", "grp"), None), P(None, "grp"))
    return jax.shard_map(per_device, mesh=mesh, in_specs=in_specs, out_specs=out_specs, check_vma=False)
```
